32 devices in a mesh: clips: 2 (over x), seq: 8 (over z, y), head: 2 (over core).
Axes of the slice: x: 2, y: 2, z: 4, core: 2. Of those that a mesh axis runs over, the one named last changes fastest.
Arguments:
- video_q: bfloat16 [2048, 2048], P(('clips', 'seq'), 'head'), parts along dimension 0, may hold values from -105 to 105
- video_k: bfloat16 [2048, 2048], P(('clips', 'seq'), 'head'), parts along dimension 0, may hold values from -5 to 5
- video_v: bfloat16 [2048, 2048], P(('clips', 'seq'), 'head'), parts along dimension 0, may hold values from -6 to 6
- audio_q: bfloat16 [512, 2048], P(('clips', 'seq'), 'head'), parts along dimension 0, may hold values from -105 to 105
- audio_k: bfloat16 [512, 2048], P(('clips', 'seq'), 'head'), parts along dimension 0, may hold values from -5 to 5
- audio_v: bfloat16 [512, 2048], P(('clips', 'seq'), 'head'), parts along dimension 0, may hold values from -6 to 6
- video_query_gain: float32 [2048], P('head'), may hold values from 1 to 2
- video_key_gain: float32 [2048], P('head'), may hold values from 1 to 2
- audio_query_gain: float32 [2048], P('head'), may hold values from 1 to 2
- audio_key_gain: float32 [2048], P('head'), may hold values from 1 to 2
Outputs:
- video_mixed: bfloat16 [2048, 2048], P(('clips', 'seq'), 'head'), parts along dimension 0
- audio_mixed: bfloat16 [512, 2048], P(('clips', 'seq'), 'head'), parts along dimension 0
The draws below stay inside these ranges and needn't reach their ends.
There are 2 independent parts, one for each index of `clips`. The reference program is written for one: setup_inputs(seed, part) draws one part's arguments, and reference() takes and returns one part's arrays. A program takes and returns all parts, laid end to end along the dimension named above; an argument that names none is the same for every part. Nothing has to cross between parts.
All inputs are finite; a program needn't handle non-finite values.
Results may differ from the reference program's by a relative error of at most 0.02.
Values may be sent and summed in bfloat16 or wider, within the bound.
No kernel may reach another device: no remote copies, remote signals or barrier semaphores. Data moves between devices by JAX's collectives and lax.ppermute only.
A program may use at most 128 MiB of HBM per device.

```python
import math
import jax
import jax.numpy as jnp
from jax import lax

HEAD_DIM = 128
VIDEO_HEADS = 16
AUDIO_HEADS = 16
VTOKENS = 1024
ATOKENS = 256


def aligned_pair(key, row_count, col_count):
    queries = jnp.clip(jax.random.normal(jax.random.fold_in(key, 31), (row_count, col_count), jnp.float32), -4.0, 4.0) * 1.25
    key_rows = jnp.clip(jax.random.normal(jax.random.fold_in(key, 37), (row_count, col_count), jnp.float32), -4.0, 4.0) * 1.25
    key_rows = key_rows.at[0, 0].set(5.0)
    key_rows = key_rows.at[1, 1].set(-5.0)
    return (queries, key_rows)


def draw_video_q(key, part):
    return aligned_pair(key, VTOKENS, VIDEO_HEADS * HEAD_DIM)[0].astype(jnp.bfloat16)


def draw_video_k(key, part):
    return aligned_pair(key, VTOKENS, VIDEO_HEADS * HEAD_DIM)[1].astype(jnp.bfloat16)


def draw_audio_q(key, part):
    return aligned_pair(key, ATOKENS, AUDIO_HEADS * HEAD_DIM)[0].astype(jnp.bfloat16)


def draw_audio_k(key, part):
    return aligned_pair(key, ATOKENS, AUDIO_HEADS * HEAD_DIM)[1].astype(jnp.bfloat16)


def steps_of(key, shape, pieces, low, high):
    loudness, own = 1.0, jax.random.fold_in(key, 6)
    for dim, parts in pieces:
        heights = jnp.exp(jax.random.uniform(jax.random.fold_in(own, dim), (parts,), jnp.float32, low / len(pieces), high / len(pieces)))
        loudness = loudness * jnp.repeat(heights, shape[dim] // parts).reshape([-1 if axis == dim else 1 for axis in range(len(shape))])
    return loudness


def bell_draw(key, extent, deviation, most, cuts=(), kind=jnp.bfloat16):
    array = jax.random.normal(key, extent, jnp.float32) * deviation
    if len(cuts) > 0:
        array = steps_of(key, extent, cuts, -0.22, 0.18) * array
    return jnp.clip(array, min=-most, max=most).astype(kind)


def setup_inputs(seed: int = 0, part: int = 0) -> dict:
    seeds = jax.random.split(jax.random.key(seed), 11)
    own_keys = jax.random.split(jax.random.fold_in(seeds[10], part), 11)
    video_q = draw_video_q(jax.random.fold_in(jax.random.fold_in(seeds[10], part), 71), part)
    video_k = draw_video_k(jax.random.fold_in(jax.random.fold_in(seeds[10], part), 71), part)
    video_v = bell_draw(own_keys[2], (VTOKENS, VIDEO_HEADS * HEAD_DIM), 1.0, 6.0, ((0, 8), (1, 2)))
    audio_q = draw_audio_q(jax.random.fold_in(jax.random.fold_in(seeds[10], part), 71), part)
    audio_k = draw_audio_k(jax.random.fold_in(jax.random.fold_in(seeds[10], part), 71), part)
    audio_v = bell_draw(own_keys[5], (ATOKENS, AUDIO_HEADS * HEAD_DIM), 1.0, 6.0, ((0, 8), (1, 2)))
    video_query_gain = jnp.clip(jnp.exp(math.log(2.0) - 0.6931472 * jax.random.uniform(seeds[6], (VIDEO_HEADS * HEAD_DIM,), jnp.float32) ** steps_of(seeds[6], (VIDEO_HEADS * HEAD_DIM,), ((0, 2),), -0.2, 0.2)), 1.0, 2.0)
    video_key_gain = jnp.clip(jnp.exp(math.log(2.0) - 0.6931472 * jax.random.uniform(seeds[7], (VIDEO_HEADS * HEAD_DIM,), jnp.float32) ** steps_of(seeds[7], (VIDEO_HEADS * HEAD_DIM,), ((0, 2),), -0.2, 0.2)), 1.0, 2.0)
    audio_query_gain = jnp.clip(jnp.exp(math.log(2.0) - 0.6931472 * jax.random.uniform(seeds[8], (AUDIO_HEADS * HEAD_DIM,), jnp.float32) ** steps_of(seeds[8], (AUDIO_HEADS * HEAD_DIM,), ((0, 2),), -0.2, 0.2)), 1.0, 2.0)
    audio_key_gain = jnp.clip(jnp.exp(math.log(2.0) - 0.6931472 * jax.random.uniform(seeds[9], (AUDIO_HEADS * HEAD_DIM,), jnp.float32) ** steps_of(seeds[9], (AUDIO_HEADS * HEAD_DIM,), ((0, 2),), -0.2, 0.2)), 1.0, 2.0)
    return dict(video_q=video_q, video_k=video_k, video_v=video_v, audio_q=audio_q, audio_k=audio_k, audio_v=audio_v, video_query_gain=video_query_gain, video_key_gain=video_key_gain, audio_query_gain=audio_query_gain, audio_key_gain=audio_key_gain)


def softmax_attend(queries, key_rows, values, head_count):
    query_count = queries.shape[0]

    def per_head(index):
        offset = (index * HEAD_DIM).astype(jnp.int32)
        left = lax.dynamic_slice_in_dim(queries, offset, HEAD_DIM, 1)
        right = lax.dynamic_slice_in_dim(key_rows, offset, HEAD_DIM, 1)
        value_cols = lax.dynamic_slice_in_dim(values, offset, HEAD_DIM, 1)
        scores = jnp.dot(left, right.T, preferred_element_type=jnp.float32) * HEAD_DIM ** (-0.5)
        weights = jnp.exp(scores - lax.optimization_barrier(jnp.max(scores, axis=1, keepdims=True)))
        row_total = lax.optimization_barrier(jnp.sum(weights, axis=1))
        output = jnp.dot(weights.astype(jnp.bfloat16), value_cols, preferred_element_type=jnp.float32)
        return output / row_total[:, None]
    stacked = lax.map(per_head, jnp.arange(head_count, dtype=jnp.int32))
    return jnp.transpose(stacked, (1, 0, 2)).reshape(query_count, head_count * HEAD_DIM)

def normed(tokens, gain_row):
    count = tokens.shape[0]
    head_count = tokens.shape[1] // HEAD_DIM
    entries = tokens.astype(jnp.float32).reshape(count, head_count, HEAD_DIM)
    scaled = entries * lax.rsqrt(lax.optimization_barrier(jnp.mean(entries * entries, axis=2, keepdims=True)) + 1e-06)
    return (scaled.reshape(count, head_count * HEAD_DIM) * gain_row).astype(jnp.bfloat16)

def reference(video_q, video_k, video_v, audio_q, audio_k, audio_v, video_query_gain, video_key_gain, audio_query_gain, audio_key_gain):
    video_self = softmax_attend(video_q, video_k, video_v, VIDEO_HEADS).astype(jnp.bfloat16)
    audio_self = softmax_attend(audio_q, audio_k, audio_v, AUDIO_HEADS).astype(jnp.bfloat16)
    video_cross = softmax_attend(normed(video_self, video_query_gain), normed(audio_self, audio_key_gain), audio_self, VIDEO_HEADS)
    audio_cross = softmax_attend(normed(audio_self, audio_query_gain), normed(video_self, video_key_gain), video_self, AUDIO_HEADS)
    video_mixed = (video_self.astype(jnp.float32) + video_cross).astype(jnp.bfloat16)
    audio_mixed = (audio_self.astype(jnp.float32) + audio_cross).astype(jnp.bfloat16)
    return (video_mixed, audio_mixed)
```

```python
import functools
import math

import jax
import jax.numpy as jnp
from jax import lax
from jax.experimental import pallas as pl
from jax.experimental.pallas import tpu as pltpu
from jax.sharding import PartitionSpec as P

HEAD_DIM = 128
SCALE = HEAD_DIM ** (-0.5)
SCALE_LOG2 = SCALE * math.log2(math.e)
VMEM_LIMIT = 48 * 1024 * 1024
ROW_CHUNK = 256


def normed(tokens, gain_row):
    count = tokens.shape[0]
    head_count = tokens.shape[1] // HEAD_DIM
    entries = tokens.astype(jnp.float32).reshape(count, head_count, HEAD_DIM)
    scaled = entries * lax.rsqrt(jnp.mean(entries * entries, axis=2, keepdims=True) + 1e-06)
    return (scaled.reshape(count, head_count * HEAD_DIM) * gain_row).astype(jnp.bfloat16)


def as_heads(tokens):
    return tokens.reshape(tokens.shape[0], tokens.shape[1] // HEAD_DIM, HEAD_DIM)


def attend(queries, key_rows, values):
    queries, key_rows, values = as_heads(queries), as_heads(key_rows), as_heads(values)
    scores = SCALE * jnp.einsum("qhd,khd->hqk", queries, key_rows, preferred_element_type=jnp.float32)
    weights = jnp.exp(scores - jnp.max(scores, axis=2, keepdims=True))
    total = jnp.sum(weights, axis=2)
    result = jnp.einsum("hqk,khd->qhd", weights.astype(jnp.bfloat16), values, preferred_element_type=jnp.float32)
    result = result / total.T[:, :, None]
    return result.reshape(result.shape[0], result.shape[1] * HEAD_DIM)


def gather_plan(vq, vk, vv, aq, ak, av, vq_gain, vk_gain, aq_gain, ak_gain):
    whole = functools.partial(lax.all_gather, axis_name="seq", axis=0, tiled=True)
    video_self = attend(vq, whole(vk), whole(vv)).astype(jnp.bfloat16)
    audio_self = attend(aq, whole(ak), whole(av)).astype(jnp.bfloat16)
    video_all, audio_all = whole(video_self), whole(audio_self)
    video_cross = attend(normed(video_self, vq_gain), normed(audio_all, ak_gain), audio_all)
    audio_cross = attend(normed(audio_self, aq_gain), normed(video_all, vk_gain), video_all)
    return (
        (video_self.astype(jnp.float32) + video_cross).astype(jnp.bfloat16),
        (audio_self.astype(jnp.float32) + audio_cross).astype(jnp.bfloat16),
    )


def partners(size):
    if size & (size - 1) == 0:
        return [[(a, a ^ step) for a in range(size)] for step in range(size)]
    return [[(a, (a + step) % size) for a in range(size)] for step in range(size)]


def partner_of(me, step, size):
    return me ^ step if size & (size - 1) == 0 else lax.rem(me + step, size)


def pack_kernel(size, *refs):
    ins, outs = refs[:6], refs[6:]
    me = lax.axis_index("seq")
    width = ins[0].shape[1] // size
    for step, out in enumerate(outs):
        column = pl.multiple_of(partner_of(me, step, size) * width, HEAD_DIM)
        row = 0
        for ref in ins:
            out[pl.ds(row, ref.shape[0]), :] = ref[:, pl.ds(column, width)]
            row += ref.shape[0]


def unpack_kernel(size, rows, *refs):
    blocks, (video_out, audio_out) = refs[:-2], refs[-2:]
    me = lax.axis_index("seq")
    width = video_out.shape[1] // size
    for step, block in enumerate(blocks):
        column = pl.multiple_of(partner_of(me, step, size) * width, HEAD_DIM)
        video_out[:, pl.ds(column, width)] = block[pl.ds(0, rows), :]
        audio_out[:, pl.ds(column, width)] = block[pl.ds(rows, block.shape[0] - rows), :]


def dot_t(left, right):
    return lax.dot_general(left, right, (((1,), (1,)), ((), ())), preferred_element_type=jnp.float32)


def dot(left, right):
    return jnp.dot(left, right, preferred_element_type=jnp.float32)


def self_attend(queries, key_rows, values):
    scores = dot_t(queries, key_rows)
    top = jnp.max(scores, axis=1, keepdims=True)
    weights = jnp.exp2((scores - top) * SCALE_LOG2)
    total = jnp.sum(weights, axis=1, keepdims=True)
    return dot(weights.astype(jnp.bfloat16), values) * (1.0 / total)


def cross_attend(queries, key_rows, values):
    weights = jnp.exp2(dot_t(queries, key_rows) * SCALE_LOG2)
    total = jnp.sum(weights, axis=1, keepdims=True)
    return dot(weights.astype(jnp.bfloat16), values) * (1.0 / total)


def unit_rows(tokens):
    entries = tokens.astype(jnp.float32)
    return entries * lax.rsqrt(jnp.mean(entries * entries, axis=1, keepdims=True) + 1e-06)


def attention_kernel(size, video_rows, audio_rows, *refs):
    blocks = refs[:size]
    gains = refs[size : size + 4]
    outs = refs[size + 4 : 2 * size + 4]
    vk, vv, ak, av, aq, v_self, a_self, v_query, v_key = refs[2 * size + 4 :]
    me = lax.axis_index("seq")
    heads = blocks[0].shape[1] // HEAD_DIM
    rv, ra = video_rows, audio_rows
    for head in range(heads):
        cols = pl.ds(head * HEAD_DIM, HEAD_DIM)
        vq_gain, vk_gain, aq_gain, ak_gain = [gain[pl.ds(me * heads + head, 1), :] for gain in gains]
        for step, block in enumerate(blocks):
            v_at, a_at = pl.ds(step * rv, rv), pl.ds(step * ra, ra)
            vk[v_at, :] = block[pl.ds(rv, rv), cols]
            vv[v_at, :] = block[pl.ds(2 * rv, rv), cols]
            aq[a_at, :] = block[pl.ds(3 * rv, ra), cols]
            ak[a_at, :] = block[pl.ds(3 * rv + ra, ra), cols]
            av[a_at, :] = block[pl.ds(3 * rv + 2 * ra, ra), cols]
        a_result = self_attend(aq[...], ak[...], av[...]).astype(jnp.bfloat16)
        a_self[...] = a_result
        a_unit = unit_rows(a_result)
        a_query = (a_unit * aq_gain).astype(jnp.bfloat16)
        a_key = (a_unit * ak_gain).astype(jnp.bfloat16)
        for step, block in enumerate(blocks):
            v_at = pl.ds(step * rv, rv)
            result = self_attend(block[pl.ds(0, rv), cols], vk[...], vv[...]).astype(jnp.bfloat16)
            v_self[v_at, :] = result
            unit = unit_rows(result)
            v_key[v_at, :] = (unit * vk_gain).astype(jnp.bfloat16)
            cross = cross_attend((unit * vq_gain).astype(jnp.bfloat16), a_key, a_result)
            outs[step][pl.ds(0, rv), cols] = (result.astype(jnp.float32) + cross).astype(jnp.bfloat16)
        cross = cross_attend(a_query, v_key[...], v_self[...])
        mixed = (a_result.astype(jnp.float32) + cross).astype(jnp.bfloat16)
        for step in range(size):
            outs[step][pl.ds(rv, ra), cols] = mixed[step * ra : (step + 1) * ra, :]


def head_plan(size, vq, vk, vv, aq, ak, av, *gains):
    rv, columns = vq.shape
    ra = aq.shape[0]
    width = columns // size
    tall = 3 * (rv + ra)
    params = pltpu.CompilerParams(vmem_limit_bytes=VMEM_LIMIT)
    in_vmem = pl.BlockSpec(memory_space=pltpu.VMEM)
    moves = partners(size)

    sends = pl.pallas_call(
        functools.partial(pack_kernel, size),
        out_shape=[jax.ShapeDtypeStruct((tall, width), vq.dtype)] * size,
        in_specs=[in_vmem] * 6,
        out_specs=[in_vmem] * size,
        compiler_params=params,
        name="pack",
    )(vq, vk, vv, aq, ak, av)
    blocks = [sends[0]] + [lax.ppermute(sends[step], "seq", moves[step]) for step in range(1, size)]
    gains = [gain.reshape(columns // HEAD_DIM, HEAD_DIM) for gain in gains]
    tv, ta = rv * size, ra * size
    results = pl.pallas_call(
        functools.partial(attention_kernel, size, rv, ra),
        out_shape=[jax.ShapeDtypeStruct((rv + ra, width), vq.dtype)] * size,
        in_specs=[in_vmem] * (size + 4),
        out_specs=[in_vmem] * size,
        scratch_shapes=[
            pltpu.VMEM((rows, HEAD_DIM), jnp.bfloat16) for rows in (tv, tv, ta, ta, ta, tv, ta, tv, tv)
        ],
        compiler_params=params,
        cost_estimate=pl.CostEstimate(
            flops=4 * width * (tv * tv + ta * ta + 2 * tv * ta),
            bytes_accessed=8 * tv * width,
            transcendentals=(width // HEAD_DIM) * (tv * tv + ta * ta + 2 * tv * ta),
        ),
        name="attention",
    )(*blocks, *gains)
    back = [results[0]] + [
        lax.ppermute(results[step], "seq", [(b, a) for a, b in moves[step]]) for step in range(1, size)
    ]
    return tuple(
        pl.pallas_call(
            functools.partial(unpack_kernel, size, rv),
            out_shape=[
                jax.ShapeDtypeStruct((rv, columns), vq.dtype),
                jax.ShapeDtypeStruct((ra, columns), vq.dtype),
            ],
            in_specs=[in_vmem] * size,
            out_specs=[in_vmem] * 2,
            compiler_params=params,
            name="unpack",
        )(*back)
    )


def solution(mesh):
    size = mesh.shape["seq"]

    def per_device(*args):
        heads = args[0].shape[1] // HEAD_DIM
        if heads % size == 0:
            return head_plan(size, *args)
        return gather_plan(*args)

    tokens = P(("clips", "seq"), "head")
    return jax.shard_map(
        per_device,
        mesh=mesh,
        in_specs=(tokens,) * 6 + (P("head"),) * 4,
        out_specs=(tokens, tokens),
        check_vma=False,
    )
```

```python
import functools
import math

import jax
import jax.numpy as jnp
from jax import lax
from jax.experimental import pallas as pl
from jax.experimental.pallas import tpu as pltpu
from jax.sharding import PartitionSpec as P

HEAD_DIM = 128
SCALE = HEAD_DIM ** (-0.5)
SCALE_LOG2 = SCALE * math.log2(math.e)
VMEM_LIMIT = 48 * 1024 * 1024
ROW_CHUNK = 256


def normed(tokens, gain_row):
    count = tokens.shape[0]
    head_count = tokens.shape[1] // HEAD_DIM
    entries = tokens.astype(jnp.float32).reshape(count, head_count, HEAD_DIM)
    scaled = entries * lax.rsqrt(jnp.mean(entries * entries, axis=2, keepdims=True) + 1e-06)
    return (scaled.reshape(count, head_count * HEAD_DIM) * gain_row).astype(jnp.bfloat16)


def as_heads(tokens):
    return tokens.reshape(tokens.shape[0], tokens.shape[1] // HEAD_DIM, HEAD_DIM)


def attend(queries, key_rows, values):
    queries, key_rows, values = as_heads(queries), as_heads(key_rows), as_heads(values)
    scores = SCALE * jnp.einsum("qhd,khd->hqk", queries, key_rows, preferred_element_type=jnp.float32)
    weights = jnp.exp(scores - jnp.max(scores, axis=2, keepdims=True))
    total = jnp.sum(weights, axis=2)
    result = jnp.einsum("hqk,khd->qhd", weights.astype(jnp.bfloat16), values, preferred_element_type=jnp.float32)
    result = result / total.T[:, :, None]
    return result.reshape(result.shape[0], result.shape[1] * HEAD_DIM)


def gather_plan(vq, vk, vv, aq, ak, av, vq_gain, vk_gain, aq_gain, ak_gain):
    whole = functools.partial(lax.all_gather, axis_name="seq", axis=0, tiled=True)
    video_self = attend(vq, whole(vk), whole(vv)).astype(jnp.bfloat16)
    audio_self = attend(aq, whole(ak), whole(av)).astype(jnp.bfloat16)
    video_all, audio_all = whole(video_self), whole(audio_self)
    video_cross = attend(normed(video_self, vq_gain), normed(audio_all, ak_gain), audio_all)
    audio_cross = attend(normed(audio_self, aq_gain), normed(video_all, vk_gain), video_all)
    return (
        (video_self.astype(jnp.float32) + video_cross).astype(jnp.bfloat16),
        (audio_self.astype(jnp.float32) + audio_cross).astype(jnp.bfloat16),
    )


def partners(size):
    if size & (size - 1) == 0:
        return [[(a, a ^ step) for a in range(size)] for step in range(size)]
    return [[(a, (a + step) % size) for a in range(size)] for step in range(size)]


def partner_of(me, step, size):
    return me ^ step if size & (size - 1) == 0 else lax.rem(me + step, size)


def send_order(size):
    middle = size // 2
    return sorted(range(1, size), key=lambda step: (step & (step - 1) and 1 + (step < middle), step))


def return_order(size):
    return range(size - 1, 0, -1)


def exchange(blocks, moves, order):
    return [blocks[0]] + [lax.ppermute(blocks[step], "seq", moves[step]) for step in order]


def pack_kernel(size, *refs):
    ins, outs, sem = refs[:6], refs[6:-1], refs[-1]
    me = lax.axis_index("seq")
    width = ins[0].shape[1] // size
    copies = []
    for step, out in enumerate(outs):
        column = pl.multiple_of(partner_of(me, step, size) * width, HEAD_DIM)
        row = 0
        for ref in ins:
            rows = ref.shape[0]
            copies.append(
                pltpu.make_async_copy(
                    ref.at[:, pl.ds(column, width)], out.at[pl.ds(row, rows), :], sem.at[len(copies)]
                )
            )
            row += rows
    for copy in copies:
        copy.start()
    for copy in copies:
        copy.wait()


def unpack_kernel(size, rows, *refs):
    blocks, (video_out, audio_out) = refs[:-2], refs[-2:]
    me = lax.axis_index("seq")
    width = video_out.shape[1] // size
    for step, block in zip((0, *return_order(size)), blocks):
        column = pl.multiple_of(partner_of(me, step, size) * width, HEAD_DIM)
        video_out[:, pl.ds(column, width)] = block[pl.ds(0, rows), :]
        audio_out[:, pl.ds(column, width)] = block[pl.ds(rows, block.shape[0] - rows), :]


def dot_t(left, right):
    return lax.dot_general(left, right, (((1,), (1,)), ((), ())), preferred_element_type=jnp.float32)


def dot(left, right):
    return jnp.dot(left, right, preferred_element_type=jnp.float32)


def self_attend(queries, key_rows, values):
    scores = dot_t(queries, key_rows)
    top = jnp.max(scores, axis=1, keepdims=True)
    weights = jnp.exp2((scores - top) * SCALE_LOG2)
    total = jnp.sum(weights, axis=1, keepdims=True)
    return dot(weights.astype(jnp.bfloat16), values) * (1.0 / total)


def cross_attend(queries, key_rows, values):
    weights = jnp.exp2(dot_t(queries, key_rows) * SCALE_LOG2)
    total = jnp.sum(weights, axis=1, keepdims=True)
    return dot(weights.astype(jnp.bfloat16), values) * (1.0 / total)


def unit_rows(tokens):
    entries = tokens.astype(jnp.float32)
    return entries * lax.rsqrt(jnp.mean(entries * entries, axis=1, keepdims=True) + 1e-06)


def attention_kernel(size, video_rows, audio_rows, *refs):
    blocks = refs[:size]
    gains = refs[size : size + 4]
    by_step = refs[size + 4 : 2 * size + 4]
    outs = [by_step[step] for step in (0, *send_order(size))]
    vk, vv, ak, av, aq, v_self, a_self, v_query, v_key = refs[2 * size + 4 :]
    me = lax.axis_index("seq")
    heads = blocks[0].shape[1] // HEAD_DIM
    rv, ra = video_rows, audio_rows
    for head in range(heads):
        cols = pl.ds(head * HEAD_DIM, HEAD_DIM)
        vq_gain, vk_gain, aq_gain, ak_gain = [gain[pl.ds(me * heads + head, 1), :] for gain in gains]
        for step, block in enumerate(blocks):
            v_at, a_at = pl.ds(step * rv, rv), pl.ds(step * ra, ra)
            vk[v_at, :] = block[pl.ds(rv, rv), cols]
            vv[v_at, :] = block[pl.ds(2 * rv, rv), cols]
            aq[a_at, :] = block[pl.ds(3 * rv, ra), cols]
            ak[a_at, :] = block[pl.ds(3 * rv + ra, ra), cols]
            av[a_at, :] = block[pl.ds(3 * rv + 2 * ra, ra), cols]
        a_result = self_attend(aq[...], ak[...], av[...]).astype(jnp.bfloat16)
        a_self[...] = a_result
        a_unit = unit_rows(a_result)
        a_query = (a_unit * aq_gain).astype(jnp.bfloat16)
        a_key = (a_unit * ak_gain).astype(jnp.bfloat16)
        for step, block in enumerate(blocks):
            v_at = pl.ds(step * rv, rv)
            result = self_attend(block[pl.ds(0, rv), cols], vk[...], vv[...]).astype(jnp.bfloat16)
            v_self[v_at, :] = result
            unit = unit_rows(result)
            v_key[v_at, :] = (unit * vk_gain).astype(jnp.bfloat16)
            cross = cross_attend((unit * vq_gain).astype(jnp.bfloat16), a_key, a_result)
            outs[step][pl.ds(0, rv), cols] = (result.astype(jnp.float32) + cross).astype(jnp.bfloat16)
        cross = cross_attend(a_query, v_key[...], v_self[...])
        mixed = (a_result.astype(jnp.float32) + cross).astype(jnp.bfloat16)
        for step in range(size):
            outs[step][pl.ds(rv, ra), cols] = mixed[step * ra : (step + 1) * ra, :]


def head_plan(size, vq, vk, vv, aq, ak, av, *gains):
    rv, columns = vq.shape
    ra = aq.shape[0]
    width = columns // size
    tall = 3 * (rv + ra)
    params = pltpu.CompilerParams(vmem_limit_bytes=VMEM_LIMIT)
    in_vmem = pl.BlockSpec(memory_space=pltpu.VMEM)
    moves = partners(size)

    sends = pl.pallas_call(
        functools.partial(pack_kernel, size),
        out_shape=[jax.ShapeDtypeStruct((tall, width), vq.dtype)] * size,
        in_specs=[pl.BlockSpec(memory_space=pltpu.HBM)] * 6,
        out_specs=[in_vmem] * size,
        scratch_shapes=[pltpu.SemaphoreType.DMA((6 * size,))],
        compiler_params=params,
        name="pack",
    )(*[pltpu.with_memory_space_constraint(x, pltpu.HBM) for x in (vq, vk, vv, aq, ak, av)])
    blocks = exchange(sends, moves, send_order(size))
    gains = [gain.reshape(columns // HEAD_DIM, HEAD_DIM) for gain in gains]
    tv, ta = rv * size, ra * size
    results = pl.pallas_call(
        functools.partial(attention_kernel, size, rv, ra),
        out_shape=[jax.ShapeDtypeStruct((rv + ra, width), vq.dtype)] * size,
        in_specs=[in_vmem] * (size + 4),
        out_specs=[in_vmem] * size,
        scratch_shapes=[
            pltpu.VMEM((rows, HEAD_DIM), jnp.bfloat16) for rows in (tv, tv, ta, ta, ta, tv, ta, tv, tv)
        ],
        compiler_params=params,
        cost_estimate=pl.CostEstimate(
            flops=4 * width * (tv * tv + ta * ta + 2 * tv * ta),
            bytes_accessed=8 * tv * width,
            transcendentals=(width // HEAD_DIM) * (tv * tv + ta * ta + 2 * tv * ta),
        ),
        name="attention",
    )(*blocks, *gains)
    back = exchange(results, [[(b, a) for a, b in move] for move in moves], return_order(size))
    return tuple(
        pl.pallas_call(
            functools.partial(unpack_kernel, size, rv),
            out_shape=[
                jax.ShapeDtypeStruct((rv, columns), vq.dtype),
                jax.ShapeDtypeStruct((ra, columns), vq.dtype),
            ],
            in_specs=[in_vmem] * size,
            out_specs=[in_vmem] * 2,
            compiler_params=params,
            name="unpack",
        )(*back)
    )


def solution(mesh):
    size = mesh.shape["seq"]

    def per_device(*args):
        heads = args[0].shape[1] // HEAD_DIM
        if heads % size == 0:
            return head_plan(size, *args)
        return gather_plan(*args)

    tokens = P(("clips", "seq"), "head")
    return jax.shard_map(
        per_device,
        mesh=mesh,
        in_specs=(tokens,) * 6 + (P("head"),) * 4,
        out_specs=(tokens, tokens),
        check_vma=False,
    )
```

```python
import functools
import math

import jax
import jax.numpy as jnp
from jax import lax
from jax.experimental import pallas as pl
from jax.experimental.pallas import tpu as pltpu
from jax.sharding import PartitionSpec as P

HEAD_DIM = 128
SCALE = HEAD_DIM ** (-0.5)
SCALE_LOG2 = SCALE * math.log2(math.e)
VMEM_LIMIT = 48 * 1024 * 1024
PACK_VMEM = 16 * 1024 * 1024


def normed(tokens, gain_row):
    count = tokens.shape[0]
    head_count = tokens.shape[1] // HEAD_DIM
    entries = tokens.astype(jnp.float32).reshape(count, head_count, HEAD_DIM)
    scaled = entries * lax.rsqrt(jnp.mean(entries * entries, axis=2, keepdims=True) + 1e-06)
    return (scaled.reshape(count, head_count * HEAD_DIM) * gain_row).astype(jnp.bfloat16)


def as_heads(tokens):
    return tokens.reshape(tokens.shape[0], tokens.shape[1] // HEAD_DIM, HEAD_DIM)


def attend(queries, key_rows, values):
    queries, key_rows, values = as_heads(queries), as_heads(key_rows), as_heads(values)
    scores = SCALE * jnp.einsum("qhd,khd->hqk", queries, key_rows, preferred_element_type=jnp.float32)
    weights = jnp.exp(scores - jnp.max(scores, axis=2, keepdims=True))
    total = jnp.sum(weights, axis=2)
    result = jnp.einsum("hqk,khd->qhd", weights.astype(jnp.bfloat16), values, preferred_element_type=jnp.float32)
    result = result / total.T[:, :, None]
    return result.reshape(result.shape[0], result.shape[1] * HEAD_DIM)


def gather_plan(vq, vk, vv, aq, ak, av, vq_gain, vk_gain, aq_gain, ak_gain):
    whole = functools.partial(lax.all_gather, axis_name="seq", axis=0, tiled=True)
    video_self = attend(vq, whole(vk), whole(vv)).astype(jnp.bfloat16)
    audio_self = attend(aq, whole(ak), whole(av)).astype(jnp.bfloat16)
    video_all, audio_all = whole(video_self), whole(audio_self)
    video_cross = attend(normed(video_self, vq_gain), normed(audio_all, ak_gain), audio_all)
    audio_cross = attend(normed(audio_self, aq_gain), normed(video_all, vk_gain), video_all)
    return (
        (video_self.astype(jnp.float32) + video_cross).astype(jnp.bfloat16),
        (audio_self.astype(jnp.float32) + audio_cross).astype(jnp.bfloat16),
    )


def partners(size):
    if size & (size - 1) == 0:
        return [[(a, a ^ step) for a in range(size)] for step in range(size)]
    return [[(a, (a + step) % size) for a in range(size)] for step in range(size)]


def partner_of(me, step, size):
    return me ^ step if size & (size - 1) == 0 else lax.rem(me + step, size)


def send_order(size):
    middle = size // 2

    def rank(step):
        return (step != middle, step & (step - 1) and 1 + (step < middle), step)

    return sorted(range(1, size), key=rank)


def exchange(blocks, moves, steps):
    return {step: lax.ppermute(blocks[step], "seq", moves[step]) for step in steps}


def pack_kernel(size, steps, *refs):
    ins, outs, sem = refs[:6], refs[-1 - len(steps) : -1], refs[-1]
    me = lax.axis_index("seq")
    width = ins[0].shape[1] // size
    copies = []
    for step, out in zip(steps, outs):
        column = pl.multiple_of(partner_of(me, step, size) * width, HEAD_DIM)
        row = 0
        for ref in ins:
            rows = ref.shape[0]
            copies.append(
                pltpu.make_async_copy(
                    ref.at[:, pl.ds(column, width)], out.at[pl.ds(row, rows), :], sem.at[len(copies)]
                )
            )
            row += rows
    for copy in copies:
        copy.start()
    for copy in copies:
        copy.wait()


def unpack_kernel(size, rows, steps, *refs):
    blocks, (video_out, audio_out) = refs[:-2], refs[-2:]
    me = lax.axis_index("seq")
    width = video_out.shape[1] // size
    for step, block in zip(steps, blocks):
        column = pl.multiple_of(partner_of(me, step, size) * width, HEAD_DIM)
        video_out[:, pl.ds(column, width)] = block[pl.ds(0, rows), :]
        audio_out[:, pl.ds(column, width)] = block[pl.ds(rows, block.shape[0] - rows), :]


def dot_t(left, right):
    return lax.dot_general(left, right, (((1,), (1,)), ((), ())), preferred_element_type=jnp.float32)


def weighed(weights, values_and_ones):
    product = jnp.dot(weights.astype(jnp.bfloat16), values_and_ones, preferred_element_type=jnp.float32)
    return product[:, :HEAD_DIM] * (1.0 / product[:, HEAD_DIM:])


def self_attend(queries, key_rows, values_and_ones):
    scores = dot_t(queries, key_rows)
    top = jnp.max(scores, axis=1, keepdims=True)
    return weighed(jnp.exp2((scores - top) * SCALE_LOG2), values_and_ones)


def cross_attend(queries, key_rows, values_and_ones):
    return weighed(jnp.exp2(dot_t(queries, key_rows) * SCALE_LOG2), values_and_ones)


def unit_rows(tokens):
    entries = tokens.astype(jnp.float32)
    return entries * lax.rsqrt(jnp.mean(entries * entries, axis=1, keepdims=True) + 1e-06)


def attention_kernel(size, video_rows, audio_rows, *refs):
    blocks = refs[:size]
    gain_refs = refs[size : size + 4]
    outs = refs[size + 4 : 2 * size + 4]
    vq, vk, vv, aq, ak, av, v_self, a_self, gains, sem = refs[2 * size + 4 :]
    me = lax.axis_index("seq")
    heads = blocks[0].shape[1] // HEAD_DIM
    rv, ra = video_rows, audio_rows
    copies = [
        pltpu.make_async_copy(ref, gains.at[at], sem.at[at]) for at, ref in enumerate(gain_refs)
    ]
    for copy in copies:
        copy.start()
    for values in (vv, av, v_self, a_self):
        values[:, HEAD_DIM:] = jnp.ones((values.shape[0], HEAD_DIM), jnp.bfloat16)
    for head in range(heads):
        cols = pl.ds(head * HEAD_DIM, HEAD_DIM)
        for at, block in enumerate(blocks):
            row = 0
            for whole, rows in ((vq, rv), (vk, rv), (vv, rv), (aq, ra), (ak, ra), (av, ra)):
                whole[pl.ds(at * rows, rows), :HEAD_DIM] = block[pl.ds(row, rows), cols]
                row += rows
        a_result = self_attend(aq[...], ak[...], av[...]).astype(jnp.bfloat16)
        v_result = self_attend(vq[...], vk[...], vv[...]).astype(jnp.bfloat16)
        a_self[:, :HEAD_DIM] = a_result
        v_self[:, :HEAD_DIM] = v_result
        if head == 0:
            for copy in copies:
                copy.wait()
        vq_gain, vk_gain, aq_gain, ak_gain = [gains[at, pl.ds(me * heads + head, 1), :] for at in range(4)]
        a_unit, v_unit = unit_rows(a_result), unit_rows(v_result)
        a_query, a_key = (a_unit * aq_gain).astype(jnp.bfloat16), (a_unit * ak_gain).astype(jnp.bfloat16)
        v_query, v_key = (v_unit * vq_gain).astype(jnp.bfloat16), (v_unit * vk_gain).astype(jnp.bfloat16)
        v_mixed = v_result.astype(jnp.float32) + cross_attend(v_query, a_key, a_self[...])
        a_mixed = a_result.astype(jnp.float32) + cross_attend(a_query, v_key, v_self[...])
        v_mixed, a_mixed = v_mixed.astype(jnp.bfloat16), a_mixed.astype(jnp.bfloat16)
        for at, out in enumerate(outs):
            out[pl.ds(0, rv), cols] = v_mixed[at * rv : (at + 1) * rv, :]
            out[pl.ds(rv, ra), cols] = a_mixed[at * ra : (at + 1) * ra, :]


def head_plan(size, vq, vk, vv, aq, ak, av, *gains):
    rv, columns = vq.shape
    ra = aq.shape[0]
    width = columns // size
    in_vmem = pl.BlockSpec(memory_space=pltpu.VMEM)
    in_hbm = pl.BlockSpec(memory_space=pltpu.HBM)
    moves = partners(size)

    arrays = [pltpu.with_memory_space_constraint(x, pltpu.HBM) for x in (vq, vk, vv, aq, ak, av)]
    order = [0, *send_order(size)]
    sends = pl.pallas_call(
        functools.partial(pack_kernel, size, order),
        out_shape=[jax.ShapeDtypeStruct((3 * (rv + ra), width), vq.dtype)] * size,
        in_specs=[in_hbm] * 6,
        out_specs=[in_vmem] * size,
        scratch_shapes=[pltpu.SemaphoreType.DMA((6 * size,))],
        compiler_params=pltpu.CompilerParams(vmem_limit_bytes=PACK_VMEM),
        name="pack",
    )(*arrays)
    sends = dict(zip(order, sends))
    blocks = {0: sends[0], **exchange(sends, moves, order[1:])}

    gains = [
        pltpu.with_memory_space_constraint(gain.reshape(columns // HEAD_DIM, HEAD_DIM), pltpu.HBM)
        for gain in gains
    ]
    tv, ta = rv * size, ra * size
    results = pl.pallas_call(
        functools.partial(attention_kernel, size, rv, ra),
        out_shape=[jax.ShapeDtypeStruct((rv + ra, width), vq.dtype)] * size,
        in_specs=[in_vmem] * size + [in_hbm] * 4,
        out_specs=[in_vmem] * size,
        scratch_shapes=[
            pltpu.VMEM((rows, parts * HEAD_DIM), jnp.bfloat16)
            for rows, parts in ((tv, 1), (tv, 1), (tv, 2), (ta, 1), (ta, 1), (ta, 2), (tv, 2), (ta, 2))
        ]
        + [pltpu.VMEM((4, columns // HEAD_DIM, HEAD_DIM), jnp.float32), pltpu.SemaphoreType.DMA((4,))],
        compiler_params=pltpu.CompilerParams(vmem_limit_bytes=VMEM_LIMIT),
        cost_estimate=pl.CostEstimate(
            flops=4 * width * (tv * tv + ta * ta + 2 * tv * ta),
            bytes_accessed=8 * tv * width,
            transcendentals=(width // HEAD_DIM) * (tv * tv + ta * ta + 2 * tv * ta),
        ),
        name="attention",
    )(*[blocks[step] for step in order], *gains)
    results = dict(zip(order, results))
    inverse = [[(b, a) for a, b in move] for move in moves]
    farthest_first = range(size - 1, 0, -1)
    back = [results[0], *exchange(results, inverse, farthest_first).values()]
    return tuple(
        pl.pallas_call(
            functools.partial(unpack_kernel, size, rv, (0, *farthest_first)),
            out_shape=[
                jax.ShapeDtypeStruct((rv, columns), vq.dtype),
                jax.ShapeDtypeStruct((ra, columns), vq.dtype),
            ],
            in_specs=[in_vmem] * size,
            out_specs=[in_vmem] * 2,
            compiler_params=pltpu.CompilerParams(vmem_limit_bytes=PACK_VMEM),
            name="unpack",
        )(*back)
    )


def solution(mesh):
    size = mesh.shape["seq"]

    def per_device(*args):
        heads = args[0].shape[1] // HEAD_DIM
        if heads % size == 0:
            return head_plan(size, *args)
        return gather_plan(*args)

    tokens = P(("clips", "seq"), "head")
    return jax.shard_map(
        per_device,
        mesh=mesh,
        in_specs=(tokens,) * 6 + (P("head"),) * 4,
        out_specs=(tokens, tokens),
        check_vma=False,
    )
```

```python
import functools
import math

import jax
import jax.numpy as jnp
from jax import lax
from jax.experimental import pallas as pl
from jax.experimental.pallas import tpu as pltpu
from jax.sharding import PartitionSpec as P

HEAD_DIM = 128
SCALE = HEAD_DIM ** (-0.5)
SCALE_LOG2 = SCALE * math.log2(math.e)
VMEM_LIMIT = 48 * 1024 * 1024
PACK_VMEM = 16 * 1024 * 1024


def normed(tokens, gain_row):
    count = tokens.shape[0]
    head_count = tokens.shape[1] // HEAD_DIM
    entries = tokens.astype(jnp.float32).reshape(count, head_count, HEAD_DIM)
    scaled = entries * lax.rsqrt(jnp.mean(entries * entries, axis=2, keepdims=True) + 1e-06)
    return (scaled.reshape(count, head_count * HEAD_DIM) * gain_row).astype(jnp.bfloat16)


def as_heads(tokens):
    return tokens.reshape(tokens.shape[0], tokens.shape[1] // HEAD_DIM, HEAD_DIM)


def attend(queries, key_rows, values):
    queries, key_rows, values = as_heads(queries), as_heads(key_rows), as_heads(values)
    scores = SCALE * jnp.einsum("qhd,khd->hqk", queries, key_rows, preferred_element_type=jnp.float32)
    weights = jnp.exp(scores - jnp.max(scores, axis=2, keepdims=True))
    total = jnp.sum(weights, axis=2)
    result = jnp.einsum("hqk,khd->qhd", weights.astype(jnp.bfloat16), values, preferred_element_type=jnp.float32)
    result = result / total.T[:, :, None]
    return result.reshape(result.shape[0], result.shape[1] * HEAD_DIM)


def gather_plan(vq, vk, vv, aq, ak, av, vq_gain, vk_gain, aq_gain, ak_gain):
    whole = functools.partial(lax.all_gather, axis_name="seq", axis=0, tiled=True)
    video_self = attend(vq, whole(vk), whole(vv)).astype(jnp.bfloat16)
    audio_self = attend(aq, whole(ak), whole(av)).astype(jnp.bfloat16)
    video_all, audio_all = whole(video_self), whole(audio_self)
    video_cross = attend(normed(video_self, vq_gain), normed(audio_all, ak_gain), audio_all)
    audio_cross = attend(normed(audio_self, aq_gain), normed(video_all, vk_gain), video_all)
    return (
        (video_self.astype(jnp.float32) + video_cross).astype(jnp.bfloat16),
        (audio_self.astype(jnp.float32) + audio_cross).astype(jnp.bfloat16),
    )


def partners(size):
    if size & (size - 1) == 0:
        return [[(a, a ^ step) for a in range(size)] for step in range(size)]
    return [[(a, (a + step) % size) for a in range(size)] for step in range(size)]


def partner_of(me, step, size):
    return me ^ step if size & (size - 1) == 0 else lax.rem(me + step, size)


def send_order(size):
    middle = size // 2

    def rank(step):
        return (step == size - 1, step != middle, step & (step - 1) and 1 + (step < middle), step)

    return sorted(range(1, size), key=rank)


def return_order(size):
    return range(size - 1, 0, -1)


def exchange(blocks, moves, steps):
    return {step: lax.ppermute(blocks[step], "seq", moves[step]) for step in steps}


def pack_kernel(size, steps, *refs):
    ins, outs, sem = refs[:6], refs[-1 - len(steps) : -1], refs[-1]
    me = lax.axis_index("seq")
    width = ins[0].shape[1] // size
    copies = []
    for step, out in zip(steps, outs):
        column = pl.multiple_of(partner_of(me, step, size) * width, HEAD_DIM)
        row = 0
        for ref in ins:
            rows = ref.shape[0]
            copies.append(
                pltpu.make_async_copy(
                    ref.at[:, pl.ds(column, width)], out.at[pl.ds(row, rows), :], sem.at[len(copies)]
                )
            )
            row += rows
    for copy in copies:
        copy.start()
    for copy in copies:
        copy.wait()


def unpack_kernel(size, rows, steps, *refs):
    blocks, (video_out, audio_out) = refs[:-2], refs[-2:]
    me = lax.axis_index("seq")
    width = video_out.shape[1] // size
    for step, block in zip(steps, blocks):
        column = pl.multiple_of(partner_of(me, step, size) * width, HEAD_DIM)
        video_out[:, pl.ds(column, width)] = block[pl.ds(0, rows), :]
        audio_out[:, pl.ds(column, width)] = block[pl.ds(rows, block.shape[0] - rows), :]


def dot_t(left, right):
    return lax.dot_general(left, right, (((1,), (1,)), ((), ())), preferred_element_type=jnp.float32)


def times(weights, values_and_ones):
    return jnp.dot(weights.astype(jnp.bfloat16), values_and_ones, preferred_element_type=jnp.float32)


def weighed(product):
    return product[:, :HEAD_DIM] * (1.0 / product[:, HEAD_DIM:])


def start_attend(queries, key_rows, values_and_ones):
    scores = dot_t(queries, key_rows)
    top = jnp.max(scores, axis=1, keepdims=True)
    return top, times(jnp.exp2((scores - top) * SCALE_LOG2), values_and_ones)


def more_attend(top, product, queries, key_rows, values_and_ones):
    scores = dot_t(queries, key_rows)
    new_top = jnp.maximum(top, jnp.max(scores, axis=1, keepdims=True))
    product = product * jnp.exp2((top - new_top) * SCALE_LOG2)
    return product + times(jnp.exp2((scores - new_top) * SCALE_LOG2), values_and_ones)


def cross_attend(queries, key_rows, values_and_ones):
    return weighed(times(jnp.exp2(dot_t(queries, key_rows) * SCALE_LOG2), values_and_ones))


def unit_rows(tokens):
    entries = tokens.astype(jnp.float32)
    return entries * lax.rsqrt(jnp.mean(entries * entries, axis=1, keepdims=True) + 1e-06)


def assemble(blocks, cols, wholes):
    for at, block in enumerate(blocks):
        row = 0
        for whole, rows in wholes:
            if whole is not None:
                whole[pl.ds(at * rows, rows), :HEAD_DIM] = block[pl.ds(row, rows), cols]
            row += rows


def fill_ones(*arrays):
    for values in arrays:
        values[:, HEAD_DIM:] = jnp.ones((values.shape[0], HEAD_DIM), jnp.bfloat16)


def early_kernel(rv, *refs):
    blocks, (tops, products, vq, vk, vv) = refs[:-5], refs[-5:]
    fill_ones(vv)
    for head in range(tops.shape[0]):
        assemble(blocks, pl.ds(head * HEAD_DIM, HEAD_DIM), ((vq, rv), (vk, rv), (vv, rv)))
        top, products[head] = start_attend(vq[...], vk[...], vv[...])
        tops[head] = jnp.broadcast_to(top, tops.shape[1:])


def attention_kernel(size, rv, ra, *refs):
    blocks, tops, products, gain_refs = refs[:size], refs[size], refs[size + 1], refs[size + 2 : size + 6]
    outs = refs[size + 6 : 2 * size + 6]
    vq, vk, vv, aq, ak, av, v_self, a_self, gains, sem = refs[2 * size + 6 :]
    me = lax.axis_index("seq")
    early, late = pl.ds(0, (size - 1) * rv), pl.ds((size - 1) * rv, rv)
    copies = [
        pltpu.make_async_copy(ref, gains.at[at], sem.at[at]) for at, ref in enumerate(gain_refs)
    ]
    for copy in copies:
        copy.start()
    fill_ones(vv, av, v_self, a_self)
    for head in range(tops.shape[0]):
        cols = pl.ds(head * HEAD_DIM, HEAD_DIM)
        assemble(blocks, cols, ((vq, rv), (vk, rv), (vv, rv), (aq, ra), (ak, ra), (av, ra)))
        _, product = start_attend(aq[...], ak[...], av[...])
        a_result = weighed(product).astype(jnp.bfloat16)
        a_self[:, :HEAD_DIM] = a_result
        product = more_attend(tops[head, :, :1], products[head], vq[early, :], vk[late, :], vv[late, :])
        v_self[early, :HEAD_DIM] = weighed(product).astype(jnp.bfloat16)
        _, product = start_attend(vq[late, :], vk[...], vv[...])
        v_self[late, :HEAD_DIM] = weighed(product).astype(jnp.bfloat16)
        v_result = v_self[:, :HEAD_DIM]
        if head == 0:
            for copy in copies:
                copy.wait()
        vq_gain, vk_gain, aq_gain, ak_gain = [
            gains[at, pl.ds(me * tops.shape[0] + head, 1), :] for at in range(4)
        ]
        a_unit, v_unit = unit_rows(a_result), unit_rows(v_result)
        a_query, a_key = (a_unit * aq_gain).astype(jnp.bfloat16), (a_unit * ak_gain).astype(jnp.bfloat16)
        v_query, v_key = (v_unit * vq_gain).astype(jnp.bfloat16), (v_unit * vk_gain).astype(jnp.bfloat16)
        v_mixed = v_result.astype(jnp.float32) + cross_attend(v_query, a_key, a_self[...])
        a_mixed = a_result.astype(jnp.float32) + cross_attend(a_query, v_key, v_self[...])
        v_mixed, a_mixed = v_mixed.astype(jnp.bfloat16), a_mixed.astype(jnp.bfloat16)
        for at, out in enumerate(outs):
            out[pl.ds(0, rv), cols] = v_mixed[at * rv : (at + 1) * rv, :]
            out[pl.ds(rv, ra), cols] = a_mixed[at * ra : (at + 1) * ra, :]


def head_plan(size, vq, vk, vv, aq, ak, av, *gains):
    rv, columns = vq.shape
    ra = aq.shape[0]
    width = columns // size
    in_vmem = pl.BlockSpec(memory_space=pltpu.VMEM)
    in_hbm = pl.BlockSpec(memory_space=pltpu.HBM)
    moves = partners(size)

    arrays = [pltpu.with_memory_space_constraint(x, pltpu.HBM) for x in (vq, vk, vv, aq, ak, av)]
    order = [0, *send_order(size)]
    sends = pl.pallas_call(
        functools.partial(pack_kernel, size, order),
        out_shape=[jax.ShapeDtypeStruct((3 * (rv + ra), width), vq.dtype)] * size,
        in_specs=[in_hbm] * 6,
        out_specs=[in_vmem] * size,
        scratch_shapes=[pltpu.SemaphoreType.DMA((6 * size,))],
        compiler_params=pltpu.CompilerParams(vmem_limit_bytes=PACK_VMEM),
        name="pack",
    )(*arrays)
    sends = dict(zip(order, sends))
    blocks = {0: sends[0], **exchange(sends, moves, order[1:])}

    gains = [
        pltpu.with_memory_space_constraint(gain.reshape(columns // HEAD_DIM, HEAD_DIM), pltpu.HBM)
        for gain in gains
    ]
    tv, ta, te, heads = rv * size, ra * size, rv * (size - 1), width // HEAD_DIM
    arrival = order
    arrived = [blocks[step] for step in arrival]
    tops, products = pl.pallas_call(
        functools.partial(early_kernel, rv),
        out_shape=[
            jax.ShapeDtypeStruct((heads, te, HEAD_DIM), jnp.float32),
            jax.ShapeDtypeStruct((heads, te, 2 * HEAD_DIM), jnp.float32),
        ],
        in_specs=[in_vmem] * (size - 1),
        out_specs=[in_vmem] * 2,
        scratch_shapes=[pltpu.VMEM((te, parts * HEAD_DIM), jnp.bfloat16) for parts in (1, 1, 2)],
        compiler_params=pltpu.CompilerParams(vmem_limit_bytes=VMEM_LIMIT),
        cost_estimate=pl.CostEstimate(
            flops=4 * width * te * te, bytes_accessed=8 * te * width, transcendentals=heads * te * te
        ),
        name="early",
    )(*arrived[:-1])
    results = pl.pallas_call(
        functools.partial(attention_kernel, size, rv, ra),
        out_shape=[jax.ShapeDtypeStruct((rv + ra, width), vq.dtype)] * size,
        in_specs=[in_vmem] * (size + 2) + [in_hbm] * 4,
        out_specs=[in_vmem] * size,
        scratch_shapes=[
            pltpu.VMEM((rows, parts * HEAD_DIM), jnp.bfloat16)
            for rows, parts in ((tv, 1), (tv, 1), (tv, 2), (ta, 1), (ta, 1), (ta, 2), (tv, 2), (ta, 2))
        ]
        + [pltpu.VMEM((4, columns // HEAD_DIM, HEAD_DIM), jnp.float32), pltpu.SemaphoreType.DMA((4,))],
        compiler_params=pltpu.CompilerParams(vmem_limit_bytes=VMEM_LIMIT),
        cost_estimate=pl.CostEstimate(
            flops=4 * width * (2 * tv * rv + ta * ta + 2 * tv * ta),
            bytes_accessed=8 * tv * width,
            transcendentals=heads * (2 * tv * rv + ta * ta + 2 * tv * ta),
        ),
        name="attention",
    )(*arrived, tops, products, *gains)
    results = dict(zip(arrival, results))
    inverse = [[(b, a) for a, b in move] for move in moves]
    back = [results[0], *exchange(results, inverse, return_order(size)).values()]
    return tuple(
        pl.pallas_call(
            functools.partial(unpack_kernel, size, rv, (0, *return_order(size))),
            out_shape=[
                jax.ShapeDtypeStruct((rv, columns), vq.dtype),
                jax.ShapeDtypeStruct((ra, columns), vq.dtype),
            ],
            in_specs=[in_vmem] * size,
            out_specs=[in_vmem] * 2,
            compiler_params=pltpu.CompilerParams(vmem_limit_bytes=PACK_VMEM),
            name="unpack",
        )(*back)
    )


def solution(mesh):
    size = mesh.shape["seq"]

    def per_device(*args):
        heads = args[0].shape[1] // HEAD_DIM
        if size > 1 and heads % size == 0:
            return head_plan(size, *args)
        return gather_plan(*args)

    tokens = P(("clips", "seq"), "head")
    return jax.shard_map(
        per_device,
        mesh=mesh,
        in_specs=(tokens,) * 6 + (P("head"),) * 4,
        out_specs=(tokens, tokens),
        check_vma=False,
    )
```

```python
import functools
import math

import jax
import jax.numpy as jnp
from jax import lax
from jax.experimental import pallas as pl
from jax.experimental.pallas import tpu as pltpu
from jax.sharding import PartitionSpec as P

HEAD_DIM = 128
SCALE = HEAD_DIM ** (-0.5)
SCALE_LOG2 = SCALE * math.log2(math.e)
VMEM_LIMIT = 48 * 1024 * 1024
PACK_VMEM = 16 * 1024 * 1024


def normed(tokens, gain_row):
    count = tokens.shape[0]
    head_count = tokens.shape[1] // HEAD_DIM
    entries = tokens.astype(jnp.float32).reshape(count, head_count, HEAD_DIM)
    scaled = entries * lax.rsqrt(jnp.mean(entries * entries, axis=2, keepdims=True) + 1e-06)
    return (scaled.reshape(count, head_count * HEAD_DIM) * gain_row).astype(jnp.bfloat16)


def as_heads(tokens):
    return tokens.reshape(tokens.shape[0], tokens.shape[1] // HEAD_DIM, HEAD_DIM)


def attend(queries, key_rows, values):
    queries, key_rows, values = as_heads(queries), as_heads(key_rows), as_heads(values)
    scores = SCALE * jnp.einsum("qhd,khd->hqk", queries, key_rows, preferred_element_type=jnp.float32)
    weights = jnp.exp(scores - jnp.max(scores, axis=2, keepdims=True))
    total = jnp.sum(weights, axis=2)
    result = jnp.einsum("hqk,khd->qhd", weights.astype(jnp.bfloat16), values, preferred_element_type=jnp.float32)
    result = result / total.T[:, :, None]
    return result.reshape(result.shape[0], result.shape[1] * HEAD_DIM)


def gather_plan(vq, vk, vv, aq, ak, av, vq_gain, vk_gain, aq_gain, ak_gain):
    whole = functools.partial(lax.all_gather, axis_name="seq", axis=0, tiled=True)
    video_self = attend(vq, whole(vk), whole(vv)).astype(jnp.bfloat16)
    audio_self = attend(aq, whole(ak), whole(av)).astype(jnp.bfloat16)
    video_all, audio_all = whole(video_self), whole(audio_self)
    video_cross = attend(normed(video_self, vq_gain), normed(audio_all, ak_gain), audio_all)
    audio_cross = attend(normed(audio_self, aq_gain), normed(video_all, vk_gain), video_all)
    return (
        (video_self.astype(jnp.float32) + video_cross).astype(jnp.bfloat16),
        (audio_self.astype(jnp.float32) + audio_cross).astype(jnp.bfloat16),
    )


def partners(size):
    if size & (size - 1) == 0:
        return [[(a, a ^ step) for a in range(size)] for step in range(size)]
    return [[(a, (a + step) % size) for a in range(size)] for step in range(size)]


def partner_of(me, step, size):
    return me ^ step if size & (size - 1) == 0 else lax.rem(me + step, size)


def send_order(size):
    middle = size // 2

    def rank(step):
        return (
            step == size - 1,
            step != middle // 2,
            step != middle,
            step & (step - 1) and 1 + (step < middle),
            step,
        )

    return sorted(range(1, size), key=rank)


def return_order(size):
    return range(size - 1, 0, -1)


def exchange(blocks, moves, steps):
    return {step: lax.ppermute(blocks[step], "seq", moves[step]) for step in steps}


def pack_kernel(size, steps, *refs):
    ins, outs, sem = refs[:6], refs[-1 - len(steps) : -1], refs[-1]
    me = lax.axis_index("seq")
    width = ins[0].shape[1] // size
    copies = []
    for step, out in zip(steps, outs):
        column = pl.multiple_of(partner_of(me, step, size) * width, HEAD_DIM)
        row = 0
        for ref in ins:
            rows = ref.shape[0]
            copies.append(
                pltpu.make_async_copy(
                    ref.at[:, pl.ds(column, width)], out.at[pl.ds(row, rows), :], sem.at[len(copies)]
                )
            )
            row += rows
    for copy in copies:
        copy.start()
    for copy in copies:
        copy.wait()


def unpack_kernel(size, rows, steps, *refs):
    blocks, (video_out, audio_out) = refs[:-2], refs[-2:]
    me = lax.axis_index("seq")
    width = video_out.shape[1] // size
    for step, block in zip(steps, blocks):
        column = pl.multiple_of(partner_of(me, step, size) * width, HEAD_DIM)
        video_out[:, pl.ds(column, width)] = block[pl.ds(0, rows), :]
        audio_out[:, pl.ds(column, width)] = block[pl.ds(rows, block.shape[0] - rows), :]


def dot_t(left, right):
    return lax.dot_general(left, right, (((1,), (1,)), ((), ())), preferred_element_type=jnp.float32)


def times(weights, values_and_ones):
    return jnp.dot(weights.astype(jnp.bfloat16), values_and_ones, preferred_element_type=jnp.float32)


def weighed(product):
    return product[:, :HEAD_DIM] * (1.0 / product[:, HEAD_DIM:])


def start_attend(queries, key_rows, values_and_ones):
    scores = dot_t(queries, key_rows)
    top = jnp.max(scores, axis=1, keepdims=True)
    return top, times(jnp.exp2((scores - top) * SCALE_LOG2), values_and_ones)


def more_attend(top, product, queries, key_rows, values_and_ones):
    scores = dot_t(queries, key_rows)
    new_top = jnp.maximum(top, jnp.max(scores, axis=1, keepdims=True))
    product = product * jnp.exp2((top - new_top) * SCALE_LOG2)
    return product + times(jnp.exp2((scores - new_top) * SCALE_LOG2), values_and_ones)


def cross_attend(queries, key_rows, values_and_ones):
    return weighed(times(jnp.exp2(dot_t(queries, key_rows) * SCALE_LOG2), values_and_ones))


def unit_rows(tokens):
    entries = tokens.astype(jnp.float32)
    return entries * lax.rsqrt(jnp.mean(entries * entries, axis=1, keepdims=True) + 1e-06)


def assemble(blocks, cols, wholes):
    for at, block in enumerate(blocks):
        row = 0
        for whole, rows in wholes:
            if whole is not None:
                whole[pl.ds(at * rows, rows), :HEAD_DIM] = block[pl.ds(row, rows), cols]
            row += rows


def fill_ones(*arrays):
    for values in arrays:
        values[:, HEAD_DIM:] = jnp.ones((values.shape[0], HEAD_DIM), jnp.bfloat16)


def early_kernel(rv, *refs):
    blocks, gain_refs, (tops, products, gains, vq, vk, vv, sem) = refs[:-11], refs[-11:-7], refs[-7:]
    copies = [pltpu.make_async_copy(ref, gains.at[at], sem.at[at]) for at, ref in enumerate(gain_refs)]
    for copy in copies:
        copy.start()
    fill_ones(vv)
    for head in range(tops.shape[0]):
        assemble(blocks, pl.ds(head * HEAD_DIM, HEAD_DIM), ((vq, rv), (vk, rv), (vv, rv)))
        top, products[head] = start_attend(vq[...], vk[...], vv[...])
        tops[head] = jnp.broadcast_to(top, tops.shape[1:])
    for copy in copies:
        copy.wait()


def attention_kernel(size, rv, ra, *refs):
    blocks, tops, products, gains = refs[:size], *refs[size : size + 3]
    outs = refs[size + 3 : 2 * size + 3]
    vq, vk, vv, aq, ak, av, v_self, a_self = refs[2 * size + 3 :]
    me = lax.axis_index("seq")
    early, late = pl.ds(0, (size - 1) * rv), pl.ds((size - 1) * rv, rv)
    fill_ones(vv, av, v_self, a_self)
    for head in range(tops.shape[0]):
        cols = pl.ds(head * HEAD_DIM, HEAD_DIM)
        assemble(blocks, cols, ((vq, rv), (vk, rv), (vv, rv), (aq, ra), (ak, ra), (av, ra)))
        _, product = start_attend(aq[...], ak[...], av[...])
        a_result = weighed(product).astype(jnp.bfloat16)
        a_self[:, :HEAD_DIM] = a_result
        product = more_attend(tops[head, :, :1], products[head], vq[early, :], vk[late, :], vv[late, :])
        v_self[early, :HEAD_DIM] = weighed(product).astype(jnp.bfloat16)
        _, product = start_attend(vq[late, :], vk[...], vv[...])
        v_self[late, :HEAD_DIM] = weighed(product).astype(jnp.bfloat16)
        v_result = v_self[:, :HEAD_DIM]
        vq_gain, vk_gain, aq_gain, ak_gain = [
            gains[at, pl.ds(me * tops.shape[0] + head, 1), :] for at in range(4)
        ]
        a_unit, v_unit = unit_rows(a_result), unit_rows(v_result)
        a_query, a_key = (a_unit * aq_gain).astype(jnp.bfloat16), (a_unit * ak_gain).astype(jnp.bfloat16)
        v_query, v_key = (v_unit * vq_gain).astype(jnp.bfloat16), (v_unit * vk_gain).astype(jnp.bfloat16)
        v_mixed = v_result.astype(jnp.float32) + cross_attend(v_query, a_key, a_self[...])
        a_mixed = a_result.astype(jnp.float32) + cross_attend(a_query, v_key, v_self[...])
        v_mixed, a_mixed = v_mixed.astype(jnp.bfloat16), a_mixed.astype(jnp.bfloat16)
        for at, out in enumerate(outs):
            out[pl.ds(0, rv), cols] = v_mixed[at * rv : (at + 1) * rv, :]
            out[pl.ds(rv, ra), cols] = a_mixed[at * ra : (at + 1) * ra, :]


def head_plan(size, vq, vk, vv, aq, ak, av, *gains):
    rv, columns = vq.shape
    ra = aq.shape[0]
    width = columns // size
    in_vmem = pl.BlockSpec(memory_space=pltpu.VMEM)
    in_hbm = pl.BlockSpec(memory_space=pltpu.HBM)
    moves = partners(size)

    arrays = [pltpu.with_memory_space_constraint(x, pltpu.HBM) for x in (vq, vk, vv, aq, ak, av)]
    order = [0, *send_order(size)]
    sends = pl.pallas_call(
        functools.partial(pack_kernel, size, order),
        out_shape=[jax.ShapeDtypeStruct((3 * (rv + ra), width), vq.dtype)] * size,
        in_specs=[in_hbm] * 6,
        out_specs=[in_vmem] * size,
        scratch_shapes=[pltpu.SemaphoreType.DMA((6 * size,))],
        compiler_params=pltpu.CompilerParams(vmem_limit_bytes=PACK_VMEM),
        name="pack",
    )(*arrays)
    sends = dict(zip(order, sends))
    blocks = {0: sends[0], **exchange(sends, moves, order[1:])}

    gains = [
        pltpu.with_memory_space_constraint(gain.reshape(columns // HEAD_DIM, HEAD_DIM), pltpu.HBM)
        for gain in gains
    ]
    tv, ta, te, heads = rv * size, ra * size, rv * (size - 1), width // HEAD_DIM
    arrived = [blocks[step] for step in order]
    tops, products, gains = pl.pallas_call(
        functools.partial(early_kernel, rv),
        out_shape=[
            jax.ShapeDtypeStruct((heads, te, HEAD_DIM), jnp.float32),
            jax.ShapeDtypeStruct((heads, te, 2 * HEAD_DIM), jnp.float32),
            jax.ShapeDtypeStruct((4, *gains[0].shape), jnp.float32),
        ],
        in_specs=[in_vmem] * (size - 1) + [in_hbm] * 4,
        out_specs=[in_vmem] * 3,
        scratch_shapes=[pltpu.VMEM((te, parts * HEAD_DIM), jnp.bfloat16) for parts in (1, 1, 2)]
        + [pltpu.SemaphoreType.DMA((4,))],
        compiler_params=pltpu.CompilerParams(vmem_limit_bytes=VMEM_LIMIT),
        cost_estimate=pl.CostEstimate(
            flops=4 * width * te * te, bytes_accessed=8 * te * width, transcendentals=heads * te * te
        ),
        name="early",
    )(*arrived[:-1], *gains)
    results = pl.pallas_call(
        functools.partial(attention_kernel, size, rv, ra),
        out_shape=[jax.ShapeDtypeStruct((rv + ra, width), vq.dtype)] * size,
        in_specs=[in_vmem] * (size + 3),
        out_specs=[in_vmem] * size,
        scratch_shapes=[
            pltpu.VMEM((rows, parts * HEAD_DIM), jnp.bfloat16)
            for rows, parts in ((tv, 1), (tv, 1), (tv, 2), (ta, 1), (ta, 1), (ta, 2), (tv, 2), (ta, 2))
        ],
        compiler_params=pltpu.CompilerParams(vmem_limit_bytes=VMEM_LIMIT),
        cost_estimate=pl.CostEstimate(
            flops=4 * width * (2 * tv * rv + ta * ta + 2 * tv * ta),
            bytes_accessed=8 * tv * width,
            transcendentals=heads * (2 * tv * rv + ta * ta + 2 * tv * ta),
        ),
        name="attention",
    )(*arrived, tops, products, gains)
    results = dict(zip(order, results))
    inverse = [[(b, a) for a, b in move] for move in moves]
    back = [results[0], *exchange(results, inverse, return_order(size)).values()]
    return tuple(
        pl.pallas_call(
            functools.partial(unpack_kernel, size, rv, (0, *return_order(size))),
            out_shape=[
                jax.ShapeDtypeStruct((rv, columns), vq.dtype),
                jax.ShapeDtypeStruct((ra, columns), vq.dtype),
            ],
            in_specs=[in_vmem] * size,
            out_specs=[in_vmem] * 2,
            compiler_params=pltpu.CompilerParams(vmem_limit_bytes=PACK_VMEM),
            name="unpack",
        )(*back)
    )


def solution(mesh):
    size = mesh.shape["seq"]

    def per_device(*args):
        heads = args[0].shape[1] // HEAD_DIM
        if size > 1 and heads % size == 0:
            return head_plan(size, *args)
        return gather_plan(*args)

    tokens = P(("clips", "seq"), "head")
    return jax.shard_map(
        per_device,
        mesh=mesh,
        in_specs=(tokens,) * 6 + (P("head"),) * 4,
        out_specs=(tokens, tokens),
        check_vma=False,
    )
```

```python
import functools
import math

import jax
import jax.numpy as jnp
from jax import lax
from jax.experimental import pallas as pl
from jax.experimental.pallas import tpu as pltpu
from jax.sharding import PartitionSpec as P

HEAD_DIM = 128
SCALE = HEAD_DIM ** (-0.5)
SCALE_LOG2 = SCALE * math.log2(math.e)
VMEM_LIMIT = 48 * 1024 * 1024
PACK_VMEM = 16 * 1024 * 1024


def normed(tokens, gain_row):
    count = tokens.shape[0]
    head_count = tokens.shape[1] // HEAD_DIM
    entries = tokens.astype(jnp.float32).reshape(count, head_count, HEAD_DIM)
    scaled = entries * lax.rsqrt(jnp.mean(entries * entries, axis=2, keepdims=True) + 1e-06)
    return (scaled.reshape(count, head_count * HEAD_DIM) * gain_row).astype(jnp.bfloat16)


def as_heads(tokens):
    return tokens.reshape(tokens.shape[0], tokens.shape[1] // HEAD_DIM, HEAD_DIM)


def attend(queries, key_rows, values):
    queries, key_rows, values = as_heads(queries), as_heads(key_rows), as_heads(values)
    scores = SCALE * jnp.einsum("qhd,khd->hqk", queries, key_rows, preferred_element_type=jnp.float32)
    weights = jnp.exp(scores - jnp.max(scores, axis=2, keepdims=True))
    total = jnp.sum(weights, axis=2)
    result = jnp.einsum("hqk,khd->qhd", weights.astype(jnp.bfloat16), values, preferred_element_type=jnp.float32)
    result = result / total.T[:, :, None]
    return result.reshape(result.shape[0], result.shape[1] * HEAD_DIM)


def gather_plan(vq, vk, vv, aq, ak, av, vq_gain, vk_gain, aq_gain, ak_gain):
    whole = functools.partial(lax.all_gather, axis_name="seq", axis=0, tiled=True)
    video_self = attend(vq, whole(vk), whole(vv)).astype(jnp.bfloat16)
    audio_self = attend(aq, whole(ak), whole(av)).astype(jnp.bfloat16)
    video_all, audio_all = whole(video_self), whole(audio_self)
    video_cross = attend(normed(video_self, vq_gain), normed(audio_all, ak_gain), audio_all)
    audio_cross = attend(normed(audio_self, aq_gain), normed(video_all, vk_gain), video_all)
    return (
        (video_self.astype(jnp.float32) + video_cross).astype(jnp.bfloat16),
        (audio_self.astype(jnp.float32) + audio_cross).astype(jnp.bfloat16),
    )


def partners(size):
    if size & (size - 1) == 0:
        return [[(a, a ^ step) for a in range(size)] for step in range(size)]
    return [[(a, (a + step) % size) for a in range(size)] for step in range(size)]


def partner_of(me, step, size):
    return me ^ step if size & (size - 1) == 0 else lax.rem(me + step, size)


def send_order(size):
    middle = size // 2

    def rank(step):
        return (
            step == size - 1,
            step != middle // 2,
            step != middle,
            step & (step - 1) and 1 + (step < middle),
            step,
        )

    return sorted(range(1, size), key=rank)


def return_order(size):
    return range(size - 1, 0, -1)


def exchange(blocks, moves, steps):
    return {step: lax.ppermute(blocks[step], "seq", moves[step]) for step in steps}


def pack_kernel(size, steps, *refs):
    ins, outs, sem = refs[:6], refs[-1 - len(steps) : -1], refs[-1]
    me = lax.axis_index("seq")
    width = ins[0].shape[1] // size
    copies = []
    for step, out in zip(steps, outs):
        column = pl.multiple_of(partner_of(me, step, size) * width, HEAD_DIM)
        row = 0
        for ref in ins:
            rows = ref.shape[0]
            copies.append(
                pltpu.make_async_copy(
                    ref.at[:, pl.ds(column, width)], out.at[pl.ds(row, rows), :], sem.at[len(copies)]
                )
            )
            row += rows
    for copy in copies:
        copy.start()
    for copy in copies:
        copy.wait()


def unpack_kernel(size, rows, steps, *refs):
    blocks, (video_out, audio_out) = refs[:-2], refs[-2:]
    me = lax.axis_index("seq")
    width = video_out.shape[1] // size
    for step, block in zip(steps, blocks):
        column = pl.multiple_of(partner_of(me, step, size) * width, HEAD_DIM)
        video_out[:, pl.ds(column, width)] = block[pl.ds(0, rows), :]
        audio_out[:, pl.ds(column, width)] = block[pl.ds(rows, block.shape[0] - rows), :]


def dot_t(left, right):
    return lax.dot_general(left, right, (((1,), (1,)), ((), ())), preferred_element_type=jnp.float32)


def times(weights, values_and_ones):
    return jnp.dot(weights.astype(jnp.bfloat16), values_and_ones, preferred_element_type=jnp.float32)


def weighed(product):
    return product[:, :HEAD_DIM] * (1.0 / product[:, HEAD_DIM:])


def start_attend(queries, key_rows, values_and_ones):
    scores = dot_t(queries, key_rows)
    top = jnp.max(scores, axis=1, keepdims=True)
    return top, times(jnp.exp2((scores - top) * SCALE_LOG2), values_and_ones)


def across(column, width):
    if column.shape[1] == 1:
        return jnp.broadcast_to(column, (column.shape[0], width))
    return jnp.concatenate([column] * pl.cdiv(width, column.shape[1]), axis=1)[:, :width]


def more_attend(top, product, queries, key_rows, values_and_ones):
    scores = dot_t(queries, key_rows)
    new_top = jnp.maximum(top, across(jnp.max(scores, axis=1, keepdims=True), top.shape[1]))
    weights = jnp.exp2((scores - across(new_top, scores.shape[1])) * SCALE_LOG2)
    product = product * across(jnp.exp2((top - new_top) * SCALE_LOG2), product.shape[1])
    return product + times(weights, values_and_ones)


def cross_attend(queries, key_rows, values_and_ones):
    return weighed(times(jnp.exp2(dot_t(queries, key_rows) * SCALE_LOG2), values_and_ones))


def unit_rows(tokens):
    entries = tokens.astype(jnp.float32)
    return entries * lax.rsqrt(jnp.mean(entries * entries, axis=1, keepdims=True) + 1e-06)


def assemble(blocks, cols, wholes):
    for at, block in enumerate(blocks):
        row = 0
        for whole, rows in wholes:
            if whole is not None:
                whole[pl.ds(at * rows, rows), :HEAD_DIM] = block[pl.ds(row, rows), cols]
            row += rows


def fill_ones(*arrays):
    for values in arrays:
        values[:, HEAD_DIM:] = jnp.ones((values.shape[0], HEAD_DIM), jnp.bfloat16)


def early_kernel(rv, *refs):
    blocks, gain_refs, (tops, products, gains, vq, vk, vv, sem) = refs[:-11], refs[-11:-7], refs[-7:]
    copies = [pltpu.make_async_copy(ref, gains.at[at], sem.at[at]) for at, ref in enumerate(gain_refs)]
    for copy in copies:
        copy.start()
    fill_ones(vv)
    for head in range(tops.shape[0]):
        assemble(blocks, pl.ds(head * HEAD_DIM, HEAD_DIM), ((vq, rv), (vk, rv), (vv, rv)))
        top, products[head] = start_attend(vq[...], vk[...], vv[...])
        tops[head] = jnp.broadcast_to(top, tops.shape[1:])
    for copy in copies:
        copy.wait()


def attention_kernel(size, rv, ra, *refs):
    blocks, tops, products, gains = refs[:size], *refs[size : size + 3]
    outs = refs[size + 3 : 2 * size + 3]
    vq, vk, vv, aq, ak, av, v_self, a_self = refs[2 * size + 3 :]
    me = lax.axis_index("seq")
    early, late = pl.ds(0, (size - 1) * rv), pl.ds((size - 1) * rv, rv)
    fill_ones(vv, av, v_self, a_self)
    for head in range(tops.shape[0]):
        cols = pl.ds(head * HEAD_DIM, HEAD_DIM)
        assemble(blocks, cols, ((vq, rv), (vk, rv), (vv, rv), (aq, ra), (ak, ra), (av, ra)))
        _, product = start_attend(aq[...], ak[...], av[...])
        a_result = weighed(product).astype(jnp.bfloat16)
        a_self[:, :HEAD_DIM] = a_result
        product = more_attend(tops[head], products[head], vq[early, :], vk[late, :], vv[late, :])
        v_self[early, :HEAD_DIM] = weighed(product).astype(jnp.bfloat16)
        _, product = start_attend(vq[late, :], vk[...], vv[...])
        v_self[late, :HEAD_DIM] = weighed(product).astype(jnp.bfloat16)
        v_result = v_self[:, :HEAD_DIM]
        vq_gain, vk_gain, aq_gain, ak_gain = [
            gains[at, pl.ds(me * tops.shape[0] + head, 1), :] for at in range(4)
        ]
        a_unit, v_unit = unit_rows(a_result), unit_rows(v_result)
        a_query, a_key = (a_unit * aq_gain).astype(jnp.bfloat16), (a_unit * ak_gain).astype(jnp.bfloat16)
        v_query, v_key = (v_unit * vq_gain).astype(jnp.bfloat16), (v_unit * vk_gain).astype(jnp.bfloat16)
        v_mixed = v_result.astype(jnp.float32) + cross_attend(v_query, a_key, a_self[...])
        a_mixed = a_result.astype(jnp.float32) + cross_attend(a_query, v_key, v_self[...])
        v_mixed, a_mixed = v_mixed.astype(jnp.bfloat16), a_mixed.astype(jnp.bfloat16)
        for at, out in enumerate(outs):
            out[pl.ds(0, rv), cols] = v_mixed[at * rv : (at + 1) * rv, :]
            out[pl.ds(rv, ra), cols] = a_mixed[at * ra : (at + 1) * ra, :]


def head_plan(size, vq, vk, vv, aq, ak, av, *gains):
    rv, columns = vq.shape
    ra = aq.shape[0]
    width = columns // size
    in_vmem = pl.BlockSpec(memory_space=pltpu.VMEM)
    in_hbm = pl.BlockSpec(memory_space=pltpu.HBM)
    moves = partners(size)

    arrays = [pltpu.with_memory_space_constraint(x, pltpu.HBM) for x in (vq, vk, vv, aq, ak, av)]
    order = [0, *send_order(size)]
    sends = pl.pallas_call(
        functools.partial(pack_kernel, size, order),
        out_shape=[jax.ShapeDtypeStruct((3 * (rv + ra), width), vq.dtype)] * size,
        in_specs=[in_hbm] * 6,
        out_specs=[in_vmem] * size,
        scratch_shapes=[pltpu.SemaphoreType.DMA((6 * size,))],
        compiler_params=pltpu.CompilerParams(vmem_limit_bytes=PACK_VMEM),
        name="pack",
    )(*arrays)
    sends = dict(zip(order, sends))
    blocks = {0: sends[0], **exchange(sends, moves, order[1:])}

    gains = [
        pltpu.with_memory_space_constraint(gain.reshape(columns // HEAD_DIM, HEAD_DIM), pltpu.HBM)
        for gain in gains
    ]
    tv, ta, te, heads = rv * size, ra * size, rv * (size - 1), width // HEAD_DIM
    arrived = [blocks[step] for step in order]
    tops, products, gains = pl.pallas_call(
        functools.partial(early_kernel, rv),
        out_shape=[
            jax.ShapeDtypeStruct((heads, te, HEAD_DIM), jnp.float32),
            jax.ShapeDtypeStruct((heads, te, 2 * HEAD_DIM), jnp.float32),
            jax.ShapeDtypeStruct((4, *gains[0].shape), jnp.float32),
        ],
        in_specs=[in_vmem] * (size - 1) + [in_hbm] * 4,
        out_specs=[in_vmem] * 3,
        scratch_shapes=[pltpu.VMEM((te, parts * HEAD_DIM), jnp.bfloat16) for parts in (1, 1, 2)]
        + [pltpu.SemaphoreType.DMA((4,))],
        compiler_params=pltpu.CompilerParams(vmem_limit_bytes=VMEM_LIMIT),
        cost_estimate=pl.CostEstimate(
            flops=4 * width * te * te, bytes_accessed=8 * te * width, transcendentals=heads * te * te
        ),
        name="early",
    )(*arrived[:-1], *gains)
    results = pl.pallas_call(
        functools.partial(attention_kernel, size, rv, ra),
        out_shape=[jax.ShapeDtypeStruct((rv + ra, width), vq.dtype)] * size,
        in_specs=[in_vmem] * (size + 3),
        out_specs=[in_vmem] * size,
        scratch_shapes=[
            pltpu.VMEM((rows, parts * HEAD_DIM), jnp.bfloat16)
            for rows, parts in ((tv, 1), (tv, 1), (tv, 2), (ta, 1), (ta, 1), (ta, 2), (tv, 2), (ta, 2))
        ],
        compiler_params=pltpu.CompilerParams(vmem_limit_bytes=VMEM_LIMIT),
        cost_estimate=pl.CostEstimate(
            flops=4 * width * (2 * tv * rv + ta * ta + 2 * tv * ta),
            bytes_accessed=8 * tv * width,
            transcendentals=heads * (2 * tv * rv + ta * ta + 2 * tv * ta),
        ),
        name="attention",
    )(*arrived, tops, products, gains)
    results = dict(zip(order, results))
    inverse = [[(b, a) for a, b in move] for move in moves]
    back = [results[0], *exchange(results, inverse, return_order(size)).values()]
    return tuple(
        pl.pallas_call(
            functools.partial(unpack_kernel, size, rv, (0, *return_order(size))),
            out_shape=[
                jax.ShapeDtypeStruct((rv, columns), vq.dtype),
                jax.ShapeDtypeStruct((ra, columns), vq.dtype),
            ],
            in_specs=[in_vmem] * size,
            out_specs=[in_vmem] * 2,
            compiler_params=pltpu.CompilerParams(vmem_limit_bytes=PACK_VMEM),
            name="unpack",
        )(*back)
    )


def solution(mesh):
    size = mesh.shape["seq"]

    def per_device(*args):
        heads = args[0].shape[1] // HEAD_DIM
        if size > 1 and heads % size == 0:
            return head_plan(size, *args)
        return gather_plan(*args)

    tokens = P(("clips", "seq"), "head")
    return jax.shard_map(
        per_device,
        mesh=mesh,
        in_specs=(tokens,) * 6 + (P("head"),) * 4,
        out_specs=(tokens, tokens),
        check_vma=False,
    )
```

```python
import functools
import math

import jax
import jax.numpy as jnp
from jax import lax
from jax.experimental import pallas as pl
from jax.experimental.pallas import tpu as pltpu
from jax.sharding import PartitionSpec as P

HEAD_DIM = 128
SCALE = HEAD_DIM ** (-0.5)
SCALE_LOG2 = SCALE * math.log2(math.e)
VMEM_LIMIT = 48 * 1024 * 1024
SOON = 5
PACK_VMEM = 16 * 1024 * 1024


def normed(tokens, gain_row):
    count = tokens.shape[0]
    head_count = tokens.shape[1] // HEAD_DIM
    entries = tokens.astype(jnp.float32).reshape(count, head_count, HEAD_DIM)
    scaled = entries * lax.rsqrt(jnp.mean(entries * entries, axis=2, keepdims=True) + 1e-06)
    return (scaled.reshape(count, head_count * HEAD_DIM) * gain_row).astype(jnp.bfloat16)


def as_heads(tokens):
    return tokens.reshape(tokens.shape[0], tokens.shape[1] // HEAD_DIM, HEAD_DIM)


def attend(queries, key_rows, values):
    queries, key_rows, values = as_heads(queries), as_heads(key_rows), as_heads(values)
    scores = SCALE * jnp.einsum("qhd,khd->hqk", queries, key_rows, preferred_element_type=jnp.float32)
    weights = jnp.exp(scores - jnp.max(scores, axis=2, keepdims=True))
    total = jnp.sum(weights, axis=2)
    result = jnp.einsum("hqk,khd->qhd", weights.astype(jnp.bfloat16), values, preferred_element_type=jnp.float32)
    result = result / total.T[:, :, None]
    return result.reshape(result.shape[0], result.shape[1] * HEAD_DIM)


def gather_plan(vq, vk, vv, aq, ak, av, vq_gain, vk_gain, aq_gain, ak_gain):
    whole = functools.partial(lax.all_gather, axis_name="seq", axis=0, tiled=True)
    video_self = attend(vq, whole(vk), whole(vv)).astype(jnp.bfloat16)
    audio_self = attend(aq, whole(ak), whole(av)).astype(jnp.bfloat16)
    video_all, audio_all = whole(video_self), whole(audio_self)
    video_cross = attend(normed(video_self, vq_gain), normed(audio_all, ak_gain), audio_all)
    audio_cross = attend(normed(audio_self, aq_gain), normed(video_all, vk_gain), video_all)
    return (
        (video_self.astype(jnp.float32) + video_cross).astype(jnp.bfloat16),
        (audio_self.astype(jnp.float32) + audio_cross).astype(jnp.bfloat16),
    )


def partners(size):
    if size & (size - 1) == 0:
        return [[(a, a ^ step) for a in range(size)] for step in range(size)]
    return [[(a, (a + step) % size) for a in range(size)] for step in range(size)]


def partner_of(me, step, size):
    return me ^ step if size & (size - 1) == 0 else lax.rem(me + step, size)


def send_order(size):
    middle = size // 2

    def rank(step):
        return (
            step == size - 1,
            step != middle // 2,
            step != middle,
            step & (step - 1) and 1 + (step < middle),
            step,
        )

    return sorted(range(1, size), key=rank)


def return_order(size):
    return range(size - 1, 0, -1)


def exchange(blocks, moves, steps):
    return {step: lax.ppermute(blocks[step], "seq", moves[step]) for step in steps}


def pack_kernel(size, steps, *refs):
    ins, outs, sem = refs[:6], refs[-1 - len(steps) : -1], refs[-1]
    me = lax.axis_index("seq")
    width = ins[0].shape[1] // size
    copies = []
    for step, out in zip(steps, outs):
        column = pl.multiple_of(partner_of(me, step, size) * width, HEAD_DIM)
        row = 0
        for ref in ins:
            rows = ref.shape[0]
            copies.append(
                pltpu.make_async_copy(
                    ref.at[:, pl.ds(column, width)], out.at[pl.ds(row, rows), :], sem.at[len(copies)]
                )
            )
            row += rows
    for copy in copies:
        copy.start()
    for copy in copies:
        copy.wait()


def unpack_kernel(size, rows, steps, *refs):
    blocks, (video_out, audio_out) = refs[:-2], refs[-2:]
    me = lax.axis_index("seq")
    width = video_out.shape[1] // size
    for step, block in zip(steps, blocks):
        column = pl.multiple_of(partner_of(me, step, size) * width, HEAD_DIM)
        video_out[:, pl.ds(column, width)] = block[pl.ds(0, rows), :]
        audio_out[:, pl.ds(column, width)] = block[pl.ds(rows, block.shape[0] - rows), :]


def dot_t(left, right):
    return lax.dot_general(left, right, (((1,), (1,)), ((), ())), preferred_element_type=jnp.float32)


def times(weights, values_and_ones):
    return jnp.dot(weights.astype(jnp.bfloat16), values_and_ones, preferred_element_type=jnp.float32)


def weighed(product):
    return product[:, :HEAD_DIM] * (1.0 / product[:, HEAD_DIM:])


def start_attend(queries, key_rows, values_and_ones):
    scores = dot_t(queries, key_rows)
    top = across(jnp.max(scores, axis=1, keepdims=True), HEAD_DIM)
    return top, times(jnp.exp2((scores - across(top, scores.shape[1])) * SCALE_LOG2), values_and_ones)


def across(column, width):
    if column.shape[1] == 1:
        return jnp.broadcast_to(column, (column.shape[0], width))
    return jnp.concatenate([column] * pl.cdiv(width, column.shape[1]), axis=1)[:, :width]


def more_attend(top, product, queries, key_rows, values_and_ones):
    scores = dot_t(queries, key_rows)
    new_top = jnp.maximum(top, across(jnp.max(scores, axis=1, keepdims=True), top.shape[1]))
    weights = jnp.exp2((scores - across(new_top, scores.shape[1])) * SCALE_LOG2)
    product = product * across(jnp.exp2((top - new_top) * SCALE_LOG2), product.shape[1])
    return product + times(weights, values_and_ones)


def cross_attend(queries, key_rows, values_and_ones):
    return weighed(times(jnp.exp2(dot_t(queries, key_rows) * SCALE_LOG2), values_and_ones))


def unit_rows(tokens):
    entries = tokens.astype(jnp.float32)
    return entries * lax.rsqrt(jnp.mean(entries * entries, axis=1, keepdims=True) + 1e-06)


def assemble(blocks, cols, wholes):
    for at, block in enumerate(blocks):
        row = 0
        for whole, rows in wholes:
            if whole is not None:
                whole[pl.ds(at * rows, rows), :HEAD_DIM] = block[pl.ds(row, rows), cols]
            row += rows


def fill_ones(*arrays):
    for values in arrays:
        values[:, HEAD_DIM:] = jnp.ones((values.shape[0], HEAD_DIM), jnp.bfloat16)


def early_kernel(rv, *refs):
    blocks, gain_refs, (tops, products, gains, vq, vk, vv, sem) = refs[:-11], refs[-11:-7], refs[-7:]
    copies = [pltpu.make_async_copy(ref, gains.at[at], sem.at[at]) for at, ref in enumerate(gain_refs)]
    for copy in copies:
        copy.start()
    fill_ones(vv)
    for head in range(tops.shape[0]):
        assemble(blocks, pl.ds(head * HEAD_DIM, HEAD_DIM), ((vq, rv), (vk, rv), (vv, rv)))
        top, products[head] = start_attend(vq[...], vk[...], vv[...])
        tops[head] = top
    for copy in copies:
        copy.wait()


def attention_kernel(size, rv, ra, *refs):
    blocks, tops, products, gains = refs[:size], *refs[size : size + 3]
    outs = refs[size + 3 : 2 * size + 3]
    vq, vk, vv, aq, ak, av, v_self, a_self = refs[2 * size + 3 :]
    me = lax.axis_index("seq")
    early, late = pl.ds(0, (size - 1) * rv), pl.ds((size - 1) * rv, rv)
    fill_ones(vv, av, v_self, a_self)
    for head in range(tops.shape[0]):
        cols = pl.ds(head * HEAD_DIM, HEAD_DIM)
        assemble(blocks, cols, ((vq, rv), (vk, rv), (vv, rv), (aq, ra), (ak, ra), (av, ra)))
        _, product = start_attend(aq[...], ak[...], av[...])
        a_result = weighed(product).astype(jnp.bfloat16)
        a_self[:, :HEAD_DIM] = a_result
        product = more_attend(tops[head], products[head], vq[early, :], vk[late, :], vv[late, :])
        v_self[early, :HEAD_DIM] = weighed(product).astype(jnp.bfloat16)
        _, product = start_attend(vq[late, :], vk[...], vv[...])
        v_self[late, :HEAD_DIM] = weighed(product).astype(jnp.bfloat16)
        v_result = v_self[:, :HEAD_DIM]
        vq_gain, vk_gain, aq_gain, ak_gain = [
            gains[at, pl.ds(me * tops.shape[0] + head, 1), :] for at in range(4)
        ]
        a_unit, v_unit = unit_rows(a_result), unit_rows(v_result)
        a_query, a_key = (a_unit * aq_gain).astype(jnp.bfloat16), (a_unit * ak_gain).astype(jnp.bfloat16)
        v_query, v_key = (v_unit * vq_gain).astype(jnp.bfloat16), (v_unit * vk_gain).astype(jnp.bfloat16)
        v_mixed = v_result.astype(jnp.float32) + cross_attend(v_query, a_key, a_self[...])
        a_mixed = a_result.astype(jnp.float32) + cross_attend(a_query, v_key, v_self[...])
        v_mixed, a_mixed = v_mixed.astype(jnp.bfloat16), a_mixed.astype(jnp.bfloat16)
        for at, out in enumerate(outs):
            out[pl.ds(0, rv), cols] = v_mixed[at * rv : (at + 1) * rv, :]
            out[pl.ds(rv, ra), cols] = a_mixed[at * ra : (at + 1) * ra, :]


def head_plan(size, vq, vk, vv, aq, ak, av, *gains):
    rv, columns = vq.shape
    ra = aq.shape[0]
    width = columns // size
    in_vmem = pl.BlockSpec(memory_space=pltpu.VMEM)
    in_hbm = pl.BlockSpec(memory_space=pltpu.HBM)
    moves = partners(size)

    arrays = [pltpu.with_memory_space_constraint(x, pltpu.HBM) for x in (vq, vk, vv, aq, ak, av)]
    order = [0, *send_order(size)]

    def pack(steps, after=()):
        return pl.pallas_call(
            functools.partial(pack_kernel, size, steps),
            out_shape=[jax.ShapeDtypeStruct((3 * (rv + ra), width), vq.dtype)] * len(steps),
            in_specs=[in_hbm] * 6 + [pl.BlockSpec(memory_space=pl.ANY)] * len(after),
            out_specs=[in_vmem] * len(steps),
            scratch_shapes=[pltpu.SemaphoreType.DMA((6 * len(steps),))],
            compiler_params=pltpu.CompilerParams(vmem_limit_bytes=PACK_VMEM),
            name="pack",
        )(*arrays, *after)

    first, rest = order[1 : 1 + SOON], [0, *order[1 + SOON :]]
    sends = dict(zip(first, pack(first)))
    blocks = exchange(sends, moves, first)
    sends.update(zip(rest, pack(rest, [blocks[first[0]]])))
    blocks.update(exchange(sends, moves, rest[1:]))
    blocks[0] = sends[0]

    gains = [
        pltpu.with_memory_space_constraint(gain.reshape(columns // HEAD_DIM, HEAD_DIM), pltpu.HBM)
        for gain in gains
    ]
    tv, ta, te, heads = rv * size, ra * size, rv * (size - 1), width // HEAD_DIM
    arrived = [blocks[step] for step in order]
    tops, products, gains = pl.pallas_call(
        functools.partial(early_kernel, rv),
        out_shape=[
            jax.ShapeDtypeStruct((heads, te, HEAD_DIM), jnp.float32),
            jax.ShapeDtypeStruct((heads, te, 2 * HEAD_DIM), jnp.float32),
            jax.ShapeDtypeStruct((4, *gains[0].shape), jnp.float32),
        ],
        in_specs=[in_vmem] * (size - 1) + [in_hbm] * 4,
        out_specs=[in_vmem] * 3,
        scratch_shapes=[pltpu.VMEM((te, parts * HEAD_DIM), jnp.bfloat16) for parts in (1, 1, 2)]
        + [pltpu.SemaphoreType.DMA((4,))],
        compiler_params=pltpu.CompilerParams(vmem_limit_bytes=VMEM_LIMIT),
        cost_estimate=pl.CostEstimate(
            flops=4 * width * te * te, bytes_accessed=8 * te * width, transcendentals=heads * te * te
        ),
        name="early",
    )(*arrived[:-1], *gains)
    results = pl.pallas_call(
        functools.partial(attention_kernel, size, rv, ra),
        out_shape=[jax.ShapeDtypeStruct((rv + ra, width), vq.dtype)] * size,
        in_specs=[in_vmem] * (size + 3),
        out_specs=[in_vmem] * size,
        scratch_shapes=[
            pltpu.VMEM((rows, parts * HEAD_DIM), jnp.bfloat16)
            for rows, parts in ((tv, 1), (tv, 1), (tv, 2), (ta, 1), (ta, 1), (ta, 2), (tv, 2), (ta, 2))
        ],
        compiler_params=pltpu.CompilerParams(vmem_limit_bytes=VMEM_LIMIT),
        cost_estimate=pl.CostEstimate(
            flops=4 * width * (2 * tv * rv + ta * ta + 2 * tv * ta),
            bytes_accessed=8 * tv * width,
            transcendentals=heads * (2 * tv * rv + ta * ta + 2 * tv * ta),
        ),
        name="attention",
    )(*arrived, tops, products, gains)
    results = dict(zip(order, results))
    inverse = [[(b, a) for a, b in move] for move in moves]
    back = [results[0], *exchange(results, inverse, return_order(size)).values()]
    return tuple(
        pl.pallas_call(
            functools.partial(unpack_kernel, size, rv, (0, *return_order(size))),
            out_shape=[
                jax.ShapeDtypeStruct((rv, columns), vq.dtype),
                jax.ShapeDtypeStruct((ra, columns), vq.dtype),
            ],
            in_specs=[in_vmem] * size,
            out_specs=[in_vmem] * 2,
            compiler_params=pltpu.CompilerParams(vmem_limit_bytes=PACK_VMEM),
            name="unpack",
        )(*back)
    )


def solution(mesh):
    size = mesh.shape["seq"]

    def per_device(*args):
        heads = args[0].shape[1] // HEAD_DIM
        if size > 1 and heads % size == 0:
            return head_plan(size, *args)
        return gather_plan(*args)

    tokens = P(("clips", "seq"), "head")
    return jax.shard_map(
        per_device,
        mesh=mesh,
        in_specs=(tokens,) * 6 + (P("head"),) * 4,
        out_specs=(tokens, tokens),
        check_vma=False,
    )
```

```python
import functools
import math

import jax
import jax.numpy as jnp
from jax import lax
from jax.experimental import pallas as pl
from jax.experimental.pallas import tpu as pltpu
from jax.sharding import PartitionSpec as P

HEAD_DIM = 128
SCALE = HEAD_DIM ** (-0.5)
SCALE_LOG2 = SCALE * math.log2(math.e)
VMEM_LIMIT = 24 * 1024 * 1024
SOON = 5
PACK_VMEM = 4 * 1024 * 1024


def normed(tokens, gain_row):
    count = tokens.shape[0]
    head_count = tokens.shape[1] // HEAD_DIM
    entries = tokens.astype(jnp.float32).reshape(count, head_count, HEAD_DIM)
    scaled = entries * lax.rsqrt(jnp.mean(entries * entries, axis=2, keepdims=True) + 1e-06)
    return (scaled.reshape(count, head_count * HEAD_DIM) * gain_row).astype(jnp.bfloat16)


def as_heads(tokens):
    return tokens.reshape(tokens.shape[0], tokens.shape[1] // HEAD_DIM, HEAD_DIM)


def attend(queries, key_rows, values):
    queries, key_rows, values = as_heads(queries), as_heads(key_rows), as_heads(values)
    scores = SCALE * jnp.einsum("qhd,khd->hqk", queries, key_rows, preferred_element_type=jnp.float32)
    weights = jnp.exp(scores - jnp.max(scores, axis=2, keepdims=True))
    total = jnp.sum(weights, axis=2)
    result = jnp.einsum("hqk,khd->qhd", weights.astype(jnp.bfloat16), values, preferred_element_type=jnp.float32)
    result = result / total.T[:, :, None]
    return result.reshape(result.shape[0], result.shape[1] * HEAD_DIM)


def gather_plan(vq, vk, vv, aq, ak, av, vq_gain, vk_gain, aq_gain, ak_gain):
    whole = functools.partial(lax.all_gather, axis_name="seq", axis=0, tiled=True)
    video_self = attend(vq, whole(vk), whole(vv)).astype(jnp.bfloat16)
    audio_self = attend(aq, whole(ak), whole(av)).astype(jnp.bfloat16)
    video_all, audio_all = whole(video_self), whole(audio_self)
    video_cross = attend(normed(video_self, vq_gain), normed(audio_all, ak_gain), audio_all)
    audio_cross = attend(normed(audio_self, aq_gain), normed(video_all, vk_gain), video_all)
    return (
        (video_self.astype(jnp.float32) + video_cross).astype(jnp.bfloat16),
        (audio_self.astype(jnp.float32) + audio_cross).astype(jnp.bfloat16),
    )


def partners(size):
    if size & (size - 1) == 0:
        return [[(a, a ^ step) for a in range(size)] for step in range(size)]
    return [[(a, (a + step) % size) for a in range(size)] for step in range(size)]


def partner_of(me, step, size):
    return me ^ step if size & (size - 1) == 0 else lax.rem(me + step, size)


def send_order(size):
    middle = size // 2

    def rank(step):
        return (
            step == size - 1,
            step != middle // 2,
            step != middle,
            step & (step - 1) and 1 + (step < middle),
            step,
        )

    return sorted(range(1, size), key=rank)


def return_order(size):
    return range(size - 1, 0, -1)


def exchange(blocks, moves, steps):
    return {step: lax.ppermute(blocks[step], "seq", moves[step]) for step in steps}


def pack_kernel(size, steps, *refs):
    ins, outs, sem = refs[:6], refs[-1 - len(steps) : -1], refs[-1]
    me = lax.axis_index("seq")
    width = ins[0].shape[1] // size
    copies = []
    for step, out in zip(steps, outs):
        column = pl.multiple_of(partner_of(me, step, size) * width, HEAD_DIM)
        row = 0
        for ref in ins:
            rows = ref.shape[0]
            copies.append(
                pltpu.make_async_copy(
                    ref.at[:, pl.ds(column, width)], out.at[pl.ds(row, rows), :], sem.at[len(copies)]
                )
            )
            row += rows
    for copy in copies:
        copy.start()
    for copy in copies:
        copy.wait()


def unpack_kernel(size, rows, steps, *refs):
    blocks, (video_out, audio_out) = refs[:-2], refs[-2:]
    me = lax.axis_index("seq")
    width = video_out.shape[1] // size
    for step, block in zip(steps, blocks):
        column = pl.multiple_of(partner_of(me, step, size) * width, HEAD_DIM)
        video_out[:, pl.ds(column, width)] = block[pl.ds(0, rows), :]
        audio_out[:, pl.ds(column, width)] = block[pl.ds(rows, block.shape[0] - rows), :]


def dot_t(left, right):
    return lax.dot_general(left, right, (((1,), (1,)), ((), ())), preferred_element_type=jnp.float32)


def times(weights, values_and_ones):
    return jnp.dot(weights.astype(jnp.bfloat16), values_and_ones, preferred_element_type=jnp.float32)


def weighed(product):
    return product[:, :HEAD_DIM] * (1.0 / product[:, HEAD_DIM:])


def start_attend(queries, key_rows, values_and_ones):
    scores = dot_t(queries, key_rows)
    top = across(jnp.max(scores, axis=1, keepdims=True), HEAD_DIM)
    return top, times(jnp.exp2((scores - across(top, scores.shape[1])) * SCALE_LOG2), values_and_ones)


def across(column, width):
    if column.shape[1] == 1:
        return jnp.broadcast_to(column, (column.shape[0], width))
    return jnp.concatenate([column] * pl.cdiv(width, column.shape[1]), axis=1)[:, :width]


def more_attend(top, product, queries, key_rows, values_and_ones):
    scores = dot_t(queries, key_rows)
    new_top = jnp.maximum(top, across(jnp.max(scores, axis=1, keepdims=True), top.shape[1]))
    weights = jnp.exp2((scores - across(new_top, scores.shape[1])) * SCALE_LOG2)
    product = product * across(jnp.exp2((top - new_top) * SCALE_LOG2), product.shape[1])
    return product + times(weights, values_and_ones)


def cross_attend(queries, key_rows, values_and_ones):
    return weighed(times(jnp.exp2(dot_t(queries, key_rows) * SCALE_LOG2), values_and_ones))


def unit_rows(tokens):
    entries = tokens.astype(jnp.float32)
    return entries * lax.rsqrt(jnp.mean(entries * entries, axis=1, keepdims=True) + 1e-06)


def assemble(blocks, cols, wholes):
    for at, block in enumerate(blocks):
        row = 0
        for whole, rows in wholes:
            if whole is not None:
                whole[pl.ds(at * rows, rows), :HEAD_DIM] = block[pl.ds(row, rows), cols]
            row += rows


def fill_ones(*arrays):
    for values in arrays:
        values[:, HEAD_DIM:] = jnp.ones((values.shape[0], HEAD_DIM), jnp.bfloat16)


def early_kernel(rv, *refs):
    blocks, gain_refs, (tops, products, gains, vq, vk, vv, sem) = refs[:-11], refs[-11:-7], refs[-7:]
    copies = [pltpu.make_async_copy(ref, gains.at[at], sem.at[at]) for at, ref in enumerate(gain_refs)]
    for copy in copies:
        copy.start()
    fill_ones(vv)
    for head in range(tops.shape[0]):
        assemble(blocks, pl.ds(head * HEAD_DIM, HEAD_DIM), ((vq, rv), (vk, rv), (vv, rv)))
        top, products[head] = start_attend(vq[...], vk[...], vv[...])
        tops[head] = top
    for copy in copies:
        copy.wait()


def attention_kernel(size, rv, ra, *refs):
    blocks, tops, products, gains = refs[:size], *refs[size : size + 3]
    outs = refs[size + 3 : 2 * size + 3]
    vq, vk, vv, aq, ak, av, v_self, a_self = refs[2 * size + 3 :]
    me = lax.axis_index("seq")
    early, late = pl.ds(0, (size - 1) * rv), pl.ds((size - 1) * rv, rv)
    fill_ones(vv, av, v_self, a_self)
    for head in range(tops.shape[0]):
        cols = pl.ds(head * HEAD_DIM, HEAD_DIM)
        assemble(blocks, cols, ((vq, rv), (vk, rv), (vv, rv), (aq, ra), (ak, ra), (av, ra)))
        _, product = start_attend(aq[...], ak[...], av[...])
        a_result = weighed(product).astype(jnp.bfloat16)
        a_self[:, :HEAD_DIM] = a_result
        product = more_attend(tops[head], products[head], vq[early, :], vk[late, :], vv[late, :])
        early_result = weighed(product).astype(jnp.bfloat16)
        _, product = start_attend(vq[late, :], vk[...], vv[...])
        v_result = jnp.concatenate([early_result, weighed(product).astype(jnp.bfloat16)], axis=0)
        v_self[:, :HEAD_DIM] = v_result
        vq_gain, vk_gain, aq_gain, ak_gain = [
            gains[at, pl.ds(me * tops.shape[0] + head, 1), :] for at in range(4)
        ]
        a_unit, v_unit = unit_rows(a_result), unit_rows(v_result)
        a_query, a_key = (a_unit * aq_gain).astype(jnp.bfloat16), (a_unit * ak_gain).astype(jnp.bfloat16)
        v_query, v_key = (v_unit * vq_gain).astype(jnp.bfloat16), (v_unit * vk_gain).astype(jnp.bfloat16)
        v_mixed = v_result.astype(jnp.float32) + cross_attend(v_query, a_key, a_self[...])
        a_mixed = a_result.astype(jnp.float32) + cross_attend(a_query, v_key, v_self[...])
        v_mixed, a_mixed = v_mixed.astype(jnp.bfloat16), a_mixed.astype(jnp.bfloat16)
        for at, out in enumerate(outs):
            out[pl.ds(0, rv), cols] = v_mixed[at * rv : (at + 1) * rv, :]
            out[pl.ds(rv, ra), cols] = a_mixed[at * ra : (at + 1) * ra, :]


def head_plan(size, vq, vk, vv, aq, ak, av, *gains):
    rv, columns = vq.shape
    ra = aq.shape[0]
    width = columns // size
    in_vmem = pl.BlockSpec(memory_space=pltpu.VMEM)
    in_hbm = pl.BlockSpec(memory_space=pltpu.HBM)
    moves = partners(size)

    arrays = [pltpu.with_memory_space_constraint(x, pltpu.HBM) for x in (vq, vk, vv, aq, ak, av)]
    order = [0, *send_order(size)]

    def pack(steps, after=()):
        return pl.pallas_call(
            functools.partial(pack_kernel, size, steps),
            out_shape=[jax.ShapeDtypeStruct((3 * (rv + ra), width), vq.dtype)] * len(steps),
            in_specs=[in_hbm] * 6 + [pl.BlockSpec(memory_space=pl.ANY)] * len(after),
            out_specs=[in_vmem] * len(steps),
            scratch_shapes=[pltpu.SemaphoreType.DMA((6 * len(steps),))],
            compiler_params=pltpu.CompilerParams(vmem_limit_bytes=PACK_VMEM),
            name="pack",
        )(*arrays, *after)

    first, rest = order[1 : 1 + SOON], [0, *order[1 + SOON :]]
    sends = dict(zip(first, pack(first)))
    blocks = exchange(sends, moves, first)
    sends.update(zip(rest, pack(rest, [blocks[first[0]]])))
    blocks.update(exchange(sends, moves, rest[1:]))
    blocks[0] = sends[0]

    gains = [
        pltpu.with_memory_space_constraint(gain.reshape(columns // HEAD_DIM, HEAD_DIM), pltpu.HBM)
        for gain in gains
    ]
    tv, ta, te, heads = rv * size, ra * size, rv * (size - 1), width // HEAD_DIM
    arrived = [blocks[step] for step in order]
    tops, products, gains = pl.pallas_call(
        functools.partial(early_kernel, rv),
        out_shape=[
            jax.ShapeDtypeStruct((heads, te, HEAD_DIM), jnp.float32),
            jax.ShapeDtypeStruct((heads, te, 2 * HEAD_DIM), jnp.float32),
            jax.ShapeDtypeStruct((4, *gains[0].shape), jnp.float32),
        ],
        in_specs=[in_vmem] * (size - 1) + [in_hbm] * 4,
        out_specs=[in_vmem] * 3,
        scratch_shapes=[pltpu.VMEM((te, parts * HEAD_DIM), jnp.bfloat16) for parts in (1, 1, 2)]
        + [pltpu.SemaphoreType.DMA((4,))],
        compiler_params=pltpu.CompilerParams(vmem_limit_bytes=VMEM_LIMIT),
        cost_estimate=pl.CostEstimate(
            flops=4 * width * te * te, bytes_accessed=8 * te * width, transcendentals=heads * te * te
        ),
        name="early",
    )(*arrived[:-1], *gains)
    results = pl.pallas_call(
        functools.partial(attention_kernel, size, rv, ra),
        out_shape=[jax.ShapeDtypeStruct((rv + ra, width), vq.dtype)] * size,
        in_specs=[in_vmem] * (size + 3),
        out_specs=[in_vmem] * size,
        scratch_shapes=[
            pltpu.VMEM((rows, parts * HEAD_DIM), jnp.bfloat16)
            for rows, parts in ((tv, 1), (tv, 1), (tv, 2), (ta, 1), (ta, 1), (ta, 2), (tv, 2), (ta, 2))
        ],
        compiler_params=pltpu.CompilerParams(vmem_limit_bytes=VMEM_LIMIT),
        cost_estimate=pl.CostEstimate(
            flops=4 * width * (2 * tv * rv + ta * ta + 2 * tv * ta),
            bytes_accessed=8 * tv * width,
            transcendentals=heads * (2 * tv * rv + ta * ta + 2 * tv * ta),
        ),
        name="attention",
    )(*arrived, tops, products, gains)
    results = dict(zip(order, results))
    inverse = [[(b, a) for a, b in move] for move in moves]
    back = [results[0], *exchange(results, inverse, return_order(size)).values()]
    return tuple(
        pl.pallas_call(
            functools.partial(unpack_kernel, size, rv, (0, *return_order(size))),
            out_shape=[
                jax.ShapeDtypeStruct((rv, columns), vq.dtype),
                jax.ShapeDtypeStruct((ra, columns), vq.dtype),
            ],
            in_specs=[in_vmem] * size,
            out_specs=[in_vmem] * 2,
            compiler_params=pltpu.CompilerParams(vmem_limit_bytes=PACK_VMEM),
            name="unpack",
        )(*back)
    )


def solution(mesh):
    size = mesh.shape["seq"]

    def per_device(*args):
        heads = args[0].shape[1] // HEAD_DIM
        if size > 1 and heads % size == 0:
            return head_plan(size, *args)
        return gather_plan(*args)

    tokens = P(("clips", "seq"), "head")
    return jax.shard_map(
        per_device,
        mesh=mesh,
        in_specs=(tokens,) * 6 + (P("head"),) * 4,
        out_specs=(tokens, tokens),
        check_vma=False,
    )
```
